512 devices in a mesh: seq: 64 (over x, z), head: 8 (over y, core).
Axes of the slice: x: 4, y: 4, z: 16, core: 2. Of those that a mesh axis runs over, the one named last changes fastest.
Arguments:
- q_raw: bfloat16 [8192, 24, 128], P('seq', 'head'), may hold values from -120 to 120
- k_raw: bfloat16 [8192, 24, 128], P('seq', 'head'), may hold values from -120 to 120
- values: bfloat16 [8192, 24, 128], P('seq', 'head'), may hold values from -6 to 6
- grad_out: bfloat16 [8192, 24, 128], P('seq', 'head'), may hold values from -6 to 6
- q_gain: float32 [24, 128], P('head'), may hold values from 0.5 to 1.5
- k_gain: float32 [24, 128], P('head'), may hold values from 0.5 to 1.5
- key_tiles: int32 [64, 13], replicated, may hold values from -1 to 63, as said below
Outputs:
- attended: bfloat16 [8192, 24, 128], P('seq', 'head')
- grad_q: bfloat16 [8192, 24, 128], P('seq', 'head')
- grad_k: bfloat16 [8192, 24, 128], P('seq', 'head')
- grad_v: bfloat16 [8192, 24, 128], P('seq', 'head')
The draws below stay inside these ranges and needn't reach their ends.
Inputs may be any that keep to these rules, and one draw needn't show every extreme that they name: `key_tiles`: frame f is the single tile f. Row r (frame f = r) lists tile f in slot 0, tile f - 1 in slot 1 and tile f + 1 in slot 2; then for each level L from 2 to 6 two slots: tile f - 2^(L-1), then tile f + 2^(L-1). An entry is -1 where that frame lies outside the clip.
All inputs are finite; a program needn't handle non-finite values.
Results may differ from the reference program's by a relative error of at most 0.03.
Values may be sent and summed in bfloat16 or wider, within the bound.
No kernel may reach another device: no remote copies, remote signals or barrier semaphores. Data moves between devices by JAX's collectives and lax.ppermute only.
A program may use at most 64 MiB of HBM per device.

```python
import jax
import jax.numpy as jnp
from jax import lax

TILE = 128
HD = 128
HEADS = 24
TOKENS = 8192
TILES_DEV = 1
LEVELS = 6
N_SEQ = 64


def head_profile(key, spread):
    order = jnp.arange(HEADS, dtype=jnp.float32) / max(HEADS - 1, 1)
    return spread ** order


def key_base(key):
    return jnp.clip(jax.random.normal(jax.random.fold_in(key, 5), (TOKENS, HEADS, HD), jnp.float32), -6.0, 6.0)


def draw_k_raw(key, part):
    base = key_base(key)
    key = jax.random.fold_in(key, 13)
    profile = head_profile(jax.random.fold_in(key, 1), 1.7320508)
    full = base * profile[None, :, None]
    return jnp.clip(full, -120.0, 120.0).astype(jnp.bfloat16)


def draw_q_raw(key, part):
    key = jax.random.fold_in(key, 17)
    noise = jnp.clip(jax.random.normal(jax.random.fold_in(key, 3), (TOKENS, HEADS, HD), jnp.float32), -6.0, 6.0)
    profile = head_profile(jax.random.fold_in(key, 1), 1.7320508)
    full = noise * profile[None, :, None]
    return jnp.clip(full, -120.0, 120.0).astype(jnp.bfloat16)


def draw_key_tiles(key, part):
    key = jax.random.fold_in(key, 31)
    frames = jnp.arange(N_SEQ, dtype=jnp.int32)
    inner = jnp.arange(TILES_DEV, dtype=jnp.int32)

    def whole_frame(other):
        inside = (other >= 0) & (other < N_SEQ)
        return jnp.where(inside[:, None], other[:, None] * TILES_DEV + inner[None, :], -1)
    columns = [whole_frame(frames), whole_frame(frames - 1), whole_frame(frames + 1)]
    for degree in range(2, LEVELS + 1):
        distance = 2 ** (degree - 1)
        for facing in (-1, 1):
            other = frames + facing * distance
            picked = jax.random.randint(jax.random.fold_in(key, 2 * degree + (facing + 1) // 2), (N_SEQ,), 0, TILES_DEV)
            inside = (other >= 0) & (other < N_SEQ)
            columns.append(jnp.where(inside, other * TILES_DEV + picked, -1)[:, None])
    table = jnp.concatenate(columns, axis=1).astype(jnp.int32)
    return jnp.repeat(table, TILES_DEV, axis=0)


def level_of(own_key, extent, shards, smallest, largest):
    level, own = 1.0, jax.random.fold_in(own_key, 6)
    for axis_at, parts in shards:
        heights = jnp.exp(jax.random.uniform(jax.random.fold_in(own, axis_at), (parts,), jnp.float32, smallest / len(shards), largest / len(shards)))
        level = level * jnp.repeat(heights, extent[axis_at] // parts).reshape([-1 if axis == axis_at else 1 for axis in range(len(extent))])
    return level


def normal_values(rng, extent, width, reach, split=(), kind=jnp.bfloat16):
    level = level_of(rng, extent, split, -0.22, 0.18) if split else 1.0
    values = jax.random.normal(rng, extent, jnp.float32) * width * level
    return jnp.minimum(jnp.maximum(values, -reach), reach).astype(kind)


def setup_inputs(seed: int = 0) -> dict:
    arg_keys = jax.random.split(jax.random.key(seed), 8)
    q_raw = draw_q_raw(jax.random.fold_in(arg_keys[7], 71), 0)
    k_raw = draw_k_raw(jax.random.fold_in(arg_keys[7], 71), 0)
    values = normal_values(arg_keys[2], (TOKENS, HEADS, HD), 1.0, 6.0, ((0, 64), (1, 8)))
    grad_out = normal_values(arg_keys[3], (TOKENS, HEADS, HD), 1.0, 6.0, ((0, 64), (1, 8)))
    q_gain = jnp.clip(1.0 + 0.1 * jax.random.normal(arg_keys[4], (HEADS, HD), jnp.float32), 0.5, 1.5)
    k_gain = jnp.clip(1.0 + 0.1 * jax.random.normal(arg_keys[5], (HEADS, HD), jnp.float32), 0.5, 1.5)
    key_tiles = draw_key_tiles(jax.random.fold_in(arg_keys[7], 71), 0)
    return dict(q_raw=q_raw, k_raw=k_raw, values=values, grad_out=grad_out, q_gain=q_gain, k_gain=k_gain, key_tiles=key_tiles)


EPS = 1e-06

def normalized(raw, gain):
    floats = raw.astype(jnp.float32)
    inverse = lax.rsqrt(lax.optimization_barrier(jnp.mean(floats * floats, axis=(1, 2))) + EPS)
    return ((floats * inverse[:, None, None] * gain[None]).astype(jnp.bfloat16), inverse)

def norm_grad(raw, gain, inverse, upstream):
    floats = raw.astype(jnp.float32)
    scaled = upstream * gain[None]
    channels = floats.shape[1] * floats.shape[2]
    inner = lax.optimization_barrier(jnp.sum(floats * scaled, axis=(1, 2)))
    result = inverse[:, None, None] * scaled - floats * (inverse ** 3 * inner / channels)[:, None, None]
    return result.astype(jnp.bfloat16)

def reference(q_raw, k_raw, values, grad_out, q_gain, k_gain, key_tiles):
    q_norm, q_inverse = normalized(q_raw, q_gain)
    k_norm, k_inverse = normalized(k_raw, k_gain)
    tokens_all, head_count, head_width = q_raw.shape
    tile_count, slot_count = key_tiles.shape
    scale = head_width ** (-0.5)
    shape_tiles = (tile_count, TILE, head_count, head_width)
    query_tiles = q_norm.reshape(shape_tiles)
    key_blocks = k_norm.reshape(shape_tiles)
    value_blocks = values.reshape(shape_tiles)
    grad_blocks = grad_out.reshape(shape_tiles)

    def per_tile(carry, tile_index):
        key_grad, value_grad = carry
        listed = key_tiles[tile_index]
        usable = listed >= 0
        clamped = jnp.where(usable, listed, 0).astype(jnp.int32)
        key_rows = key_blocks[clamped].reshape(slot_count * TILE, head_count, head_width).astype(jnp.float32)
        value_rows = value_blocks[clamped].reshape(slot_count * TILE, head_count, head_width).astype(jnp.float32)
        query_rows = query_tiles[tile_index].astype(jnp.float32)
        upstream = grad_blocks[tile_index].astype(jnp.float32)
        allowed = jnp.repeat(usable, TILE)
        score = jnp.einsum('qhd,khd->hqk', query_rows, key_rows) * scale
        score = jnp.where(allowed[None, None, :], score, -1e+30)
        weights_raw = jnp.exp(score - lax.optimization_barrier(jnp.max(score, axis=2, keepdims=True)))
        prob = weights_raw / lax.optimization_barrier(jnp.sum(weights_raw, axis=2, keepdims=True))
        prob_b = lax.optimization_barrier(prob.astype(jnp.bfloat16)).astype(jnp.float32)
        out_tile = jnp.einsum('hqk,khd->qhd', prob_b, value_rows).astype(jnp.bfloat16)
        out_back = lax.optimization_barrier(out_tile).astype(jnp.float32)
        delta = lax.optimization_barrier(jnp.sum(upstream * out_back, axis=2))
        dprob = jnp.einsum('qhd,khd->hqk', upstream, value_rows)
        dscore = prob * (dprob - jnp.transpose(delta)[:, :, None])
        dscore_b = lax.optimization_barrier(dscore.astype(jnp.bfloat16)).astype(jnp.float32)
        query_grad = jnp.einsum('hqk,khd->qhd', dscore_b, key_rows) * scale
        key_part = jnp.einsum('hqk,qhd->khd', dscore_b, query_rows) * scale
        value_part = jnp.einsum('hqk,qhd->khd', prob_b, upstream)
        weight_mask = usable.astype(key_part.dtype)[:, None, None, None]
        key_grad = key_grad.at[clamped].add(key_part.reshape(slot_count, TILE, head_count, head_width) * weight_mask)
        value_grad = value_grad.at[clamped].add(value_part.reshape(slot_count, TILE, head_count, head_width) * weight_mask)
        return ((key_grad, value_grad), (out_tile, query_grad))
    zeros = jnp.zeros(shape_tiles, jnp.float32)
    (key_grad, value_grad), (out_tiles, query_grads) = lax.scan(per_tile, (zeros, zeros), jnp.arange(tile_count, dtype=jnp.int32))
    full_shape = (tokens_all, head_count, head_width)
    attended = out_tiles.reshape(full_shape)
    grad_q = norm_grad(q_raw, q_gain, q_inverse, query_grads.reshape(full_shape))
    grad_k = norm_grad(k_raw, k_gain, k_inverse, key_grad.reshape(full_shape))
    grad_v = value_grad.reshape(full_shape).astype(jnp.bfloat16)
    return (attended, grad_q, grad_k, grad_v)
```

```python
import functools

import jax
import jax.numpy as jnp
from jax import lax
from jax.experimental import pallas as pl
from jax.experimental.pallas import tpu as pltpu
from jax.sharding import Mesh, PartitionSpec as P

TILE = 128
EPS = 1e-06
OFFSETS = (0, -1, 1, -2, 2, -4, 4, -8, 8, -16, 16, -32, 32)
NT = (((1,), (1,)), ((), ()))
NN = (((1,), (0,)), ((), ()))
F32 = jnp.float32
BF16 = jnp.bfloat16
VMEM_LIMIT = 48 * 1024 * 1024


def dot(left, right, dims):
    return lax.dot_general(left, right, dims, preferred_element_type=F32)


def row_sums(square):
    ones = jnp.ones((8, TILE), BF16)
    high = square.astype(BF16)
    low = (square - high.astype(F32)).astype(BF16)
    return dot(ones, high, NT) + dot(ones, low, NT)


def columns(rows):
    fill = jnp.zeros((TILE - rows.shape[0], TILE), F32)
    return jnp.transpose(jnp.concatenate([rows, fill], axis=0))


def squares_kernel(heads, q_ref, *refs):
    tiles, out_ref = refs[:-1], refs[-1]
    for place, ref in enumerate(tiles + (q_ref,)):
        total = jnp.zeros((TILE, TILE), F32)
        for head in range(heads):
            floats = ref[head].astype(F32)
            total = total + floats * floats
        out_ref[place : place + 1, :] = row_sums(total)[0:1]
    out_ref[len(tiles) + 1 :, :] = jnp.zeros((16 - len(tiles) - 1, TILE), F32)


def forward_kernel(
    heads, channels, listed_ref, sums_ref, q_ref, do_ref, qg_ref, kg_ref, *refs
):
    count = len(OFFSETS)
    tiles = refs[:count]
    out_ref, dq_ref, kn_ref, stat_refs = refs[count], refs[count + 1], refs[count + 2], refs[count + 3 : -3]
    norm_ref, work_ref, part_ref = refs[-3:]
    scale = TILE ** (-0.5)
    inverse = lax.rsqrt(sums_ref[...] / channels + EPS)
    turned = columns(inverse)
    usable = [listed_ref[0, t] >= 0 for t in range(count)]
    lane = lax.broadcasted_iota(jnp.int32, (TILE, TILE), 1)
    stats = jnp.zeros((TILE, TILE), F32)
    query_terms = jnp.zeros((TILE, TILE), F32)
    for head in range(heads):
        query = (
            q_ref[head].astype(F32) * turned[:, count : count + 1] * qg_ref[head : head + 1]
        ).astype(BF16)
        upstream = do_ref[head]
        top = jnp.full((TILE, TILE), -1e30, F32)
        for t in range(count):
            key = (
                tiles[t][head].astype(F32) * turned[:, t : t + 1] * kg_ref[head : head + 1]
            ).astype(BF16)
            norm_ref[t] = key
            if t == 0:
                kn_ref[head] = key
            score = dot(query, key, NT) * scale
            score = jnp.where(usable[t], score, -1e30)
            work_ref[t] = score
            top = jnp.maximum(top, score)
        top = jnp.max(top, axis=1, keepdims=True)
        total = jnp.zeros((TILE, TILE), F32)
        for t in range(count):
            total = total + jnp.exp(work_ref[t] - top)
        total = jnp.sum(total, axis=1, keepdims=True)
        level = top + jnp.log(total)
        share = 1.0 / total
        out = jnp.zeros((TILE, TILE), F32)
        for t in range(count):
            prob = jnp.exp(work_ref[t] - top) * share
            out = out + dot(prob.astype(BF16), tiles[t][heads + head], NN)
        out = out.astype(BF16)
        out_ref[head] = out
        delta = jnp.sum(
            upstream.astype(F32) * out.astype(F32), axis=1, keepdims=True
        )
        query_grad = jnp.zeros((TILE, TILE), F32)
        for t in range(count):
            score = work_ref[t]
            prob = jnp.exp(score - top) * share
            dscore = (prob * (dot(upstream, tiles[t][heads + head], NT) - delta)).astype(BF16)
            query_grad = query_grad + dot(dscore, norm_ref[t], NN)
            term = dscore.astype(F32) * score
            query_terms = query_terms + term
            term = jnp.sum(term, axis=0, keepdims=True)
            if head:
                term = term + part_ref[t : t + 1, :]
            part_ref[t : t + 1, :] = term
        dq_ref[head] = query_grad * scale
        stats = jnp.where(lane == head, level, stats)
        stats = jnp.where(lane == heads + head, delta, stats)
    query_total = jnp.sum(query_terms, axis=1, keepdims=True)
    stats = jnp.where(lane == 2 * heads + 1, query_total, stats)
    rows = jnp.transpose(stats)[0:8]
    place = lax.broadcasted_iota(jnp.int32, (8, TILE), 0)
    rows = jnp.where(place == 2 * heads, inverse[count : count + 1], rows)
    stat_refs[0][...] = rows
    for t in range(1, count):
        stat_refs[t][...] = jnp.where(place == 2 * heads + 1, part_ref[t : t + 1, :], rows)
    stat_refs[count][...] = jnp.where(
        place == 0, rows[2 * heads + 1 : 2 * heads + 2], jnp.where(place == 1, part_ref[0:1, :], 0.0)
    )


def backward_kernel(heads, listed_ref, kn_ref, v_ref, qg_ref, *refs):
    count = len(OFFSETS)
    tiles, stat_refs = refs[:count], refs[count : 2 * count]
    dk_ref, dv_ref = refs[-2:]
    scale = TILE ** (-0.5)
    turned = columns(
        jnp.concatenate([ref[2 * heads : 2 * heads + 1] for ref in stat_refs], axis=0)
    )
    usable = [listed_ref[0, t] >= 0 for t in range(count)]
    for head in range(heads):
        key, value = kn_ref[head], v_ref[head]
        key_grad = jnp.zeros((TILE, TILE), F32)
        value_grad = jnp.zeros((TILE, TILE), F32)
        for t in range(count):
            query = (
                tiles[t][head].astype(F32) * turned[:, t : t + 1] * qg_ref[head : head + 1]
            ).astype(BF16)
            upstream = tiles[t][heads + head]
            score = dot(key, query, NT) * scale - stat_refs[t][head : head + 1]
            prob = jnp.exp(jnp.where(usable[t], score, -1e30))
            value_grad = value_grad + dot(prob.astype(BF16), upstream, NN)
            dprob = dot(value, upstream, NT)
            dscore = prob * (dprob - stat_refs[t][heads + head : heads + head + 1])
            key_grad = key_grad + dot(dscore.astype(BF16), query, NN)
        dk_ref[head] = key_grad * scale
        dv_ref[head] = value_grad.astype(BF16)


def final_kernel(
    heads, channels, sums_ref, terms_ref, q_ref, k_ref, dq_ref, dk_ref, qg_ref, kg_ref, gq_ref, gk_ref
):
    count = len(OFFSETS)
    inverse = lax.rsqrt(sums_ref[...] / channels + EPS)
    squared = inverse * inverse / channels
    turned = columns(
        jnp.concatenate(
            [
                inverse[count : count + 1],
                inverse[0:1],
                squared[count : count + 1] * terms_ref[0:1],
                squared[0:1] * terms_ref[1:2],
            ],
            axis=0,
        )
    )
    for head in range(heads):
        gq_ref[head] = (
            turned[:, 0:1] * (qg_ref[head : head + 1] * dq_ref[head])
            - q_ref[head].astype(F32) * turned[:, 2:3]
        ).astype(BF16)
        gk_ref[head] = (
            turned[:, 1:2] * (kg_ref[head : head + 1] * dk_ref[head])
            - k_ref[head].astype(F32) * turned[:, 3:4]
        ).astype(BF16)


def passed(value, steps, count):
    pairs = [(i, i + steps) for i in range(count) if 0 <= i + steps < count]
    return lax.ppermute(value, "seq", pairs)


def spread(value, count):
    got = {0: value}
    for facing in (-1, 1):
        got[16 * facing] = passed(value, -16 * facing, count)
        got[32 * facing] = passed(value, -32 * facing, count)
    for distance in (1, 2, 4, 8):
        for facing in (-1, 1):
            near = distance // 2
            source = got[facing * near] if near else value
            got[facing * distance] = passed(source, -facing * (distance - near), count)
    return [got[offset] for offset in OFFSETS]


def per_device(seq_count, total_heads, q_raw, k_raw, values, grad_out, q_gain, k_gain, key_tiles):
    place = lax.axis_index("seq")
    heads = q_raw.shape[1]
    channels = float(total_heads * q_raw.shape[2])
    q_raw, k_raw, values, grad_out = [
        jnp.transpose(array, (1, 0, 2)) for array in (q_raw, k_raw, values, grad_out)
    ]
    listed = lax.dynamic_slice_in_dim(key_tiles, place, 1, 0)
    first = jnp.concatenate([k_raw, values], axis=0)
    second = jnp.concatenate([q_raw, grad_out], axis=0)
    first_all = spread(first, seq_count)
    second_all = spread(second, seq_count)

    count = len(OFFSETS)
    vmem = pl.BlockSpec(memory_space=pltpu.VMEM)
    smem = pl.BlockSpec(memory_space=pltpu.SMEM)
    params = pltpu.CompilerParams(vmem_limit_bytes=VMEM_LIMIT)
    whole = (heads, TILE, TILE)
    sums = pl.pallas_call(
        functools.partial(squares_kernel, heads),
        out_shape=jax.ShapeDtypeStruct((16, TILE), F32),
        in_specs=[vmem] * (count + 1),
        out_specs=vmem,
        compiler_params=params,
        name="squares",
    )(q_raw, *first_all)
    sums = lax.psum(lax.psum(sums, "c"), "y")
    results = pl.pallas_call(
        functools.partial(forward_kernel, heads, channels),
        out_shape=[
            jax.ShapeDtypeStruct(whole, BF16),
            jax.ShapeDtypeStruct(whole, F32),
            jax.ShapeDtypeStruct(whole, BF16),
        ]
        + [jax.ShapeDtypeStruct((8, TILE), F32)] * (count + 1),
        in_specs=[smem] + [vmem] * (5 + count),
        out_specs=[vmem] * (count + 4),
        scratch_shapes=[
            pltpu.VMEM((count, TILE, TILE), BF16),
            pltpu.VMEM((count, TILE, TILE), F32),
            pltpu.VMEM((16, TILE), F32),
        ],
        compiler_params=params,
        name="forward",
    )(listed, sums, q_raw, grad_out, q_gain, k_gain, *first_all)
    attended, dq, k_norm = results[:3]
    stats = results[3:-1]
    got_stats = [stats[0]] + [
        passed(stat, OFFSETS[t], seq_count) for t, stat in enumerate(stats) if t
    ]
    order = [OFFSETS.index(-offset) for offset in OFFSETS]
    got_stats = [got_stats[at] for at in order]
    own_terms = results[-1]
    key_total = sum(stat[2 * heads + 1] for stat in got_stats[1:]) + own_terms[1]
    terms = jnp.stack([own_terms[0], key_total])
    terms = lax.psum(lax.psum(terms, "c"), "y")
    dk, grad_v = pl.pallas_call(
        functools.partial(backward_kernel, heads),
        out_shape=[jax.ShapeDtypeStruct(whole, F32), jax.ShapeDtypeStruct(whole, BF16)],
        in_specs=[smem] + [vmem] * (3 + 2 * count),
        out_specs=[vmem] * 2,
        compiler_params=params,
        name="backward",
    )(listed, k_norm, values, q_gain, *second_all, *got_stats)
    grad_q, grad_k = pl.pallas_call(
        functools.partial(final_kernel, heads, channels),
        out_shape=[jax.ShapeDtypeStruct(whole, BF16)] * 2,
        in_specs=[vmem] * 8,
        out_specs=[vmem] * 2,
        compiler_params=params,
        name="final",
    )(sums, terms, q_raw, k_raw, dq, dk, q_gain, k_gain)
    return tuple(
        jnp.transpose(array, (1, 0, 2)) for array in (attended, grad_q, grad_k, grad_v)
    )


def solution(mesh):
    shape = dict(mesh.shape)
    cores = 2 if shape["head"] % 2 == 0 else 1
    split = Mesh(
        mesh.devices.reshape(shape["seq"], shape["head"] // cores, cores), ("seq", "y", "c")
    )
    heads = ("y", "c")

    def whole(q_raw, k_raw, values, grad_out, q_gain, k_gain, key_tiles):
        tokens = P("seq", heads, None)
        return jax.shard_map(
            functools.partial(per_device, shape["seq"], q_raw.shape[1]),
            mesh=split,
            in_specs=(tokens,) * 4 + (P(heads, None), P(heads, None), P()),
            out_specs=(tokens,) * 4,
            check_vma=False,
        )(q_raw, k_raw, values, grad_out, q_gain, k_gain, key_tiles)

    return whole
```

```python
import functools

import jax
import jax.numpy as jnp
from jax import lax
from jax.experimental import pallas as pl
from jax.experimental.pallas import tpu as pltpu
from jax.sharding import Mesh, PartitionSpec as P

TILE = 128
EPS = 1e-06
OFFSETS = (0, -1, 1, -2, 2, -4, 4, -8, 8, -16, 16, -32, 32)
NT = (((1,), (1,)), ((), ()))
NN = (((1,), (0,)), ((), ()))
F32 = jnp.float32
BF16 = jnp.bfloat16
VMEM_LIMIT = 48 * 1024 * 1024


def dot(left, right, dims):
    return lax.dot_general(left, right, dims, preferred_element_type=F32)


def row_sums(square):
    ones = jnp.ones((8, TILE), BF16)
    high = square.astype(BF16)
    low = (square - high.astype(F32)).astype(BF16)
    return dot(ones, high, NT) + dot(ones, low, NT)


def columns(rows):
    fill = jnp.zeros((TILE - rows.shape[0], TILE), F32)
    return jnp.transpose(jnp.concatenate([rows, fill], axis=0))


def tile_of(tiles, gathered_ref, frame, near, line, place, skip=0):
    if place < near:
        return lambda i: tiles[place][i]
    at = frame // line + OFFSETS[place] // line
    at = jnp.minimum(jnp.maximum(at, 0), gathered_ref.shape[0] - 1)
    return lambda i: gathered_ref[at, skip + i]


def squares_kernel(heads, near, line, listed_ref, q_ref, gathered_ref, *refs):
    tiles, out_ref = refs[:-1], refs[-1]
    count = len(OFFSETS)
    reads = [tile_of(tiles, gathered_ref, listed_ref[0, 0], near, line, t) for t in range(count)]
    reads.append(lambda i: q_ref[i])
    for place, read in enumerate(reads):
        total = jnp.zeros((TILE, TILE), F32)
        for head in range(heads):
            floats = read(head).astype(F32)
            total = total + floats * floats
        out_ref[place : place + 1, :] = row_sums(total)[0:1]
    out_ref[count + 1 :, :] = jnp.zeros((16 - count - 1, TILE), F32)


def forward_kernel(
    heads, near, line, channels, listed_ref, sums_ref, q_ref, do_ref, qg_ref, kg_ref, gathered_ref, *refs
):
    count = len(OFFSETS)
    tiles = refs[:near]
    out_ref, dq_ref, kn_ref, stat_ref, norm_ref, work_ref = refs[near:]
    scale = TILE ** (-0.5)
    inverse = lax.rsqrt(sums_ref[...] / channels + EPS)
    turned = columns(inverse)
    usable = [listed_ref[0, t] >= 0 for t in range(count)]
    reads = [tile_of(tiles, gathered_ref, listed_ref[0, 0], near, line, t) for t in range(count)]
    lane = lax.broadcasted_iota(jnp.int32, (TILE, TILE), 1)
    stats = jnp.zeros((TILE, TILE), F32)
    query_terms = jnp.zeros((TILE, TILE), F32)
    for head in range(heads):
        query = (
            q_ref[head].astype(F32) * turned[:, count : count + 1] * qg_ref[head : head + 1]
        ).astype(BF16)
        upstream = do_ref[head]
        top = jnp.full((TILE, TILE), -1e30, F32)
        for t in range(count):
            key = (
                reads[t](head).astype(F32) * turned[:, t : t + 1] * kg_ref[head : head + 1]
            ).astype(BF16)
            norm_ref[t] = key
            if t == 0:
                kn_ref[head] = key
            score = dot(query, key, NT) * scale
            score = jnp.where(usable[t], score, -1e30)
            work_ref[t] = score
            top = jnp.maximum(top, score)
        top = jnp.max(top, axis=1, keepdims=True)
        total = jnp.zeros((TILE, TILE), F32)
        for t in range(count):
            total = total + jnp.exp(work_ref[t] - top)
        total = jnp.sum(total, axis=1, keepdims=True)
        level = top + jnp.log(total)
        share = 1.0 / total
        out = jnp.zeros((TILE, TILE), F32)
        for t in range(count):
            prob = jnp.exp(work_ref[t] - top) * share
            out = out + dot(prob.astype(BF16), reads[t](heads + head), NN)
        out = out.astype(BF16)
        out_ref[head] = out
        delta = jnp.sum(
            upstream.astype(F32) * out.astype(F32), axis=1, keepdims=True
        )
        query_grad = jnp.zeros((TILE, TILE), F32)
        for t in range(count):
            score = work_ref[t]
            prob = jnp.exp(score - top) * share
            dscore = (prob * (dot(upstream, reads[t](heads + head), NT) - delta)).astype(BF16)
            query_grad = query_grad + dot(dscore, norm_ref[t], NN)
            term = dscore.astype(F32) * score
            query_terms = query_terms + term
            term = jnp.sum(term, axis=0, keepdims=True)
            if head:
                term = term + stat_ref[8 + t : 9 + t, :]
            stat_ref[8 + t : 9 + t, :] = term
        dq_ref[head] = query_grad * scale
        stats = jnp.where(lane == head, level, stats)
        stats = jnp.where(lane == heads + head, delta, stats)
    query_total = jnp.sum(query_terms, axis=1, keepdims=True)
    stats = jnp.where(lane == 2 * heads + 1, query_total, stats)
    rows = jnp.transpose(stats)[0:8]
    place = lax.broadcasted_iota(jnp.int32, (8, TILE), 0)
    stat_ref[0:8, :] = jnp.where(place == 2 * heads, inverse[count : count + 1], rows)
    stat_ref[8 + count : 9 + count, :] = rows[2 * heads + 1 : 2 * heads + 2]
    stat_ref[9 + count :, :] = jnp.zeros((24 - 9 - count, TILE), F32)


def lanes_kernel(heads, near, place_ref, stats_ref, near_ref, far_ref, terms_ref, total_ref):
    count = len(OFFSETS)
    lane, frame, half = place_ref[0], place_ref[1], place_ref[2]
    groups = stats_ref.shape[0]
    total = stats_ref[0]
    for group in range(1, groups):
        total = total + stats_ref[group]
    total_ref[...] = total
    last = 2 * heads + 1
    far = jnp.where(lane < 2, near + lane, jnp.where(frame < half, near + 3, near + 2))
    for ref, slot in ((near_ref, 1 + lane), (far_ref, far)):
        term = total_ref[pl.ds(8 + slot, 1), :]
        for group in range(groups):
            ref[group] = stats_ref[group, 0:8]
            ref[group, last : last + 1, :] = term
    terms_ref[0:1, :] = total[8 + count : 9 + count]
    terms_ref[1:2, :] = total[8:9]
    terms_ref[2:, :] = jnp.zeros((6, TILE), F32)


def backward_kernel(
    heads, near, line, channels, listed_ref, sums_ref, terms_ref, own_ref, got_ref,
    q_ref, k_ref, kn_ref, v_ref, dq_ref, qg_ref, kg_ref, gathered_ref, *refs
):
    count = len(OFFSETS)
    tiles = refs[:near]
    gq_ref, gk_ref, dv_ref = refs[near:]
    scale = TILE ** (-0.5)
    inverse_at, term_at = 2 * heads, 2 * heads + 1

    def stat(t, row):
        if t == 0:
            return own_ref[row : row + 1]
        if t < near:
            return got_ref[(t - 1) ^ 1, row : row + 1]
        lane = {0: 1, 1: 0, 2: 2, 3: 2}[t - near]
        return got_ref[lane, 8 + row : 9 + row]

    inverse = lax.rsqrt(sums_ref[...] / channels + EPS)
    squared = inverse * inverse / channels
    key_term = terms_ref[1:2]
    for t in range(1, count):
        if t != count - 1:
            key_term = key_term + stat(t, term_at)
    turned = columns(
        jnp.concatenate(
            [stat(t, inverse_at) for t in range(count)]
            + [
                inverse[0:1],
                squared[count : count + 1] * terms_ref[0:1],
                squared[0:1] * key_term,
            ],
            axis=0,
        )
    )
    usable = [listed_ref[0, t] >= 0 for t in range(count)]
    reads = [
        tile_of(tiles, gathered_ref, listed_ref[0, 0], near, line, t, 2 * heads) for t in range(count)
    ]
    for head in range(heads):
        key, value = kn_ref[head], v_ref[head]
        key_grad = jnp.zeros((TILE, TILE), F32)
        value_grad = jnp.zeros((TILE, TILE), F32)
        for t in range(count):
            query = (
                reads[t](head).astype(F32) * turned[:, t : t + 1] * qg_ref[head : head + 1]
            ).astype(BF16)
            upstream = reads[t](heads + head)
            score = dot(key, query, NT) * scale - stat(t, head)
            prob = jnp.exp(jnp.where(usable[t], score, -1e30))
            value_grad = value_grad + dot(prob.astype(BF16), upstream, NN)
            dprob = dot(value, upstream, NT)
            dscore = prob * (dprob - stat(t, heads + head))
            key_grad = key_grad + dot(dscore.astype(BF16), query, NN)
        dv_ref[head] = value_grad.astype(BF16)
        gk_ref[head] = (
            turned[:, count : count + 1] * (kg_ref[head : head + 1] * (key_grad * scale))
            - k_ref[head].astype(F32) * turned[:, count + 2 : count + 3]
        ).astype(BF16)
        gq_ref[head] = (
            turned[:, 0:1] * (qg_ref[head : head + 1] * dq_ref[head])
            - q_ref[head].astype(F32) * turned[:, count + 1 : count + 2]
        ).astype(BF16)


SEQ, HEAD = ("x", "z"), ("y", "c")


def passed(value, steps, count):
    pairs = [(i, i + steps) for i in range(count) if 0 <= i + steps < count]
    return lax.ppermute(value, SEQ, pairs)


def spread(value, count, line):
    got = {0: value}
    distance = 1
    while distance < line:
        for facing in (-1, 1):
            near = distance // 2
            source = got[facing * near]
            got[facing * distance] = passed(source, -facing * (distance - near), count)
        distance *= 2
    return [got[offset] for offset in OFFSETS if offset in got]


def per_device(total_heads, q_raw, k_raw, values, grad_out, q_gain, k_gain, key_tiles):
    lines, line = lax.axis_size("x"), lax.axis_size("z")
    seq_count = lines * line
    groups = lax.axis_size("y") * lax.axis_size("c")
    place = lax.axis_index(SEQ)
    lane = lax.axis_index(HEAD)
    heads = q_raw.shape[1]
    channels = float(total_heads * q_raw.shape[2])
    q_raw, k_raw, values, grad_out = [
        jnp.transpose(array, (1, 0, 2)) for array in (q_raw, k_raw, values, grad_out)
    ]
    listed = lax.dynamic_slice_in_dim(key_tiles, place, 1, 0)
    first = jnp.concatenate([k_raw, values], axis=0)
    second = jnp.concatenate([q_raw, grad_out], axis=0)
    column = lax.all_gather(
        jnp.concatenate([k_raw, values, q_raw, grad_out], axis=0), "x"
    )
    first_all = spread(first, seq_count, line)
    second_all = spread(second, seq_count, line)
    near = len(first_all)

    vmem = pl.BlockSpec(memory_space=pltpu.VMEM)
    smem = pl.BlockSpec(memory_space=pltpu.SMEM)
    params = pltpu.CompilerParams(vmem_limit_bytes=VMEM_LIMIT)
    whole = (heads, TILE, TILE)
    count = len(OFFSETS)
    sums = pl.pallas_call(
        functools.partial(squares_kernel, heads, near, line),
        out_shape=jax.ShapeDtypeStruct((16, TILE), F32),
        in_specs=[smem] + [vmem] * (near + 2),
        out_specs=vmem,
        compiler_params=params,
        name="squares",
    )(listed, q_raw, column, *first_all)
    sums = lax.psum(lax.psum(sums, "c"), "y")
    attended, dq, k_norm, stats = pl.pallas_call(
        functools.partial(forward_kernel, heads, near, line, channels),
        out_shape=[
            jax.ShapeDtypeStruct(whole, BF16),
            jax.ShapeDtypeStruct(whole, F32),
            jax.ShapeDtypeStruct(whole, BF16),
            jax.ShapeDtypeStruct((24, TILE), F32),
        ],
        in_specs=[smem] + [vmem] * (6 + near),
        out_specs=[vmem] * 4,
        scratch_shapes=[
            pltpu.VMEM((count, TILE, TILE), BF16),
            pltpu.VMEM((count, TILE, TILE), F32),
        ],
        compiler_params=params,
        name="forward",
    )(listed, sums, q_raw, grad_out, q_gain, k_gain, column, *first_all)

    stats, *second_all = lax.optimization_barrier((stats, *second_all))
    gathered = lax.all_gather(stats, HEAD)
    spot = jnp.stack([lane, place, jnp.int32(seq_count // 2)]).astype(jnp.int32)
    row = jax.ShapeDtypeStruct((groups, 8, TILE), F32)
    near_out, far_out, terms = pl.pallas_call(
        functools.partial(lanes_kernel, heads, near),
        out_shape=[row, row, jax.ShapeDtypeStruct((8, TILE), F32)],
        in_specs=[smem, vmem],
        out_specs=[vmem] * 3,
        scratch_shapes=[pltpu.VMEM((24, TILE), F32)],
        compiler_params=params,
        name="lanes",
    )(spot, gathered)
    near_pairs = [
        (frame * groups + at, (frame + OFFSETS[1 + at]) * groups + at)
        for frame in range(seq_count)
        for at in range(near - 1)
        if 0 <= frame + OFFSETS[1 + at] < seq_count
    ]
    far_pairs = [
        (frame * groups + at, (frame + shift) % seq_count * groups + at)
        for frame in range(seq_count)
        for at, shift in enumerate((-line, line, seq_count // 2))
        if at == 2 or 0 <= frame + shift < seq_count
    ]
    near_in = lax.ppermute(near_out, SEQ + HEAD, near_pairs)
    far_in = lax.ppermute(far_out, SEQ + HEAD, far_pairs)
    got = lax.all_to_all(
        jnp.concatenate([near_in, far_in], axis=1), HEAD, 0, 0, tiled=True
    )
    grad_q, grad_k, grad_v = pl.pallas_call(
        functools.partial(backward_kernel, heads, near, line, channels),
        out_shape=[jax.ShapeDtypeStruct(whole, BF16)] * 3,
        in_specs=[smem] + [vmem] * (12 + near),
        out_specs=[vmem] * 3,
        compiler_params=params,
        name="backward",
    )(
        listed, sums, terms, stats, got, q_raw, k_raw, k_norm, values, dq, q_gain, k_gain,
        column, *second_all,
    )
    return tuple(
        jnp.transpose(array, (1, 0, 2)) for array in (attended, grad_q, grad_k, grad_v)
    )


def solution(mesh):
    split = Mesh(mesh.devices.reshape(4, -1, mesh.shape["head"] // 2, 2), SEQ + HEAD)

    def whole(q_raw, k_raw, values, grad_out, q_gain, k_gain, key_tiles):
        tokens = P(SEQ, HEAD, None)
        return jax.shard_map(
            functools.partial(per_device, q_raw.shape[1]),
            mesh=split,
            in_specs=(tokens,) * 4 + (P(HEAD, None), P(HEAD, None), P()),
            out_specs=(tokens,) * 4,
            check_vma=False,
        )(q_raw, k_raw, values, grad_out, q_gain, k_gain, key_tiles)

    return whole
```

```python
import functools

import jax
import jax.numpy as jnp
from jax import lax
from jax.experimental import pallas as pl
from jax.experimental.pallas import tpu as pltpu
from jax.sharding import Mesh, PartitionSpec as P

TILE = 128
EPS = 1e-06
OFFSETS = (0, -1, 1, -2, 2, -4, 4, -8, 8, -16, 16, -32, 32)
NT = (((1,), (1,)), ((), ()))
NN = (((1,), (0,)), ((), ()))
F32 = jnp.float32
BF16 = jnp.bfloat16
VMEM_LIMIT = 48 * 1024 * 1024


def dot(left, right, dims):
    return lax.dot_general(left, right, dims, preferred_element_type=F32)


def row_sums(square):
    ones = jnp.ones((8, TILE), BF16)
    high = square.astype(BF16)
    low = (square - high.astype(F32)).astype(BF16)
    return dot(ones, high, NT) + dot(ones, low, NT)


def columns(rows):
    fill = jnp.zeros((TILE - rows.shape[0], TILE), F32)
    return jnp.transpose(jnp.concatenate([rows, fill], axis=0))


def own_frame():
    return lax.axis_index("x") * lax.axis_size("z") + lax.axis_index("z")


def inside(frame, line, place):
    at = frame + OFFSETS[place]
    return (at >= 0) & (at < line * lax.axis_size("x"))


def tile_of(tiles, gathered_ref, frame, near, line, place, skip=0):
    if place < near:
        return lambda i: tiles[place][i]
    at = frame // line + OFFSETS[place] // line
    at = jnp.minimum(jnp.maximum(at, 0), gathered_ref.shape[0] - 1)
    return lambda i: gathered_ref[at, skip + i]


def squares_kernel(heads, near, line, q_ref, gathered_ref, *refs):
    tiles, out_ref = refs[:-1], refs[-1]
    count = len(OFFSETS)
    frame = own_frame()
    reads = [tile_of(tiles, gathered_ref, frame, near, line, t) for t in range(count)]
    reads.append(lambda i: q_ref[i])
    for place, read in enumerate(reads):
        total = jnp.zeros((TILE, TILE), F32)
        for head in range(heads):
            floats = read(head).astype(F32)
            total = total + floats * floats
        out_ref[place : place + 1, :] = row_sums(total)[0:1]
    out_ref[count + 1 :, :] = jnp.zeros((16 - count - 1, TILE), F32)


def forward_kernel(
    heads, near, line, channels, sums_ref, q_ref, do_ref, gain_ref, gathered_ref, *refs
):
    count = len(OFFSETS)
    tiles = refs[:near]
    out_ref, dq_ref, kn_ref, stat_ref, norm_ref, work_ref = refs[near:]
    scale = TILE ** (-0.5)
    inverse = lax.rsqrt(sums_ref[...] / channels + EPS)
    turned = columns(inverse)
    frame = own_frame()
    usable = [inside(frame, line, t) for t in range(count)]
    reads = [tile_of(tiles, gathered_ref, frame, near, line, t) for t in range(count)]
    lane = lax.broadcasted_iota(jnp.int32, (TILE, TILE), 1)
    stats = jnp.zeros((TILE, TILE), F32)
    query_terms = jnp.zeros((TILE, TILE), F32)
    for head in range(heads):
        query = (
            q_ref[head].astype(F32) * turned[:, count : count + 1] * gain_ref[head : head + 1]
        ).astype(BF16)
        upstream = do_ref[head]
        top = jnp.full((TILE, TILE), -1e30, F32)
        for t in range(count):
            key = (
                reads[t](head).astype(F32) * turned[:, t : t + 1] * gain_ref[heads + head : heads + head + 1]
            ).astype(BF16)
            norm_ref[t] = key
            if t == 0:
                kn_ref[head] = key
            score = dot(query, key, NT) * scale
            score = jnp.where(usable[t], score, -1e30)
            work_ref[t] = score
            top = jnp.maximum(top, score)
        top = jnp.max(top, axis=1, keepdims=True)
        total = jnp.zeros((TILE, TILE), F32)
        for t in range(count):
            total = total + jnp.exp(work_ref[t] - top)
        total = jnp.sum(total, axis=1, keepdims=True)
        level = top + jnp.log(total)
        share = 1.0 / total
        out = jnp.zeros((TILE, TILE), F32)
        for t in range(count):
            prob = jnp.exp(work_ref[t] - top) * share
            out = out + dot(prob.astype(BF16), reads[t](heads + head), NN)
        out = out.astype(BF16)
        out_ref[head] = out
        delta = jnp.sum(
            upstream.astype(F32) * out.astype(F32), axis=1, keepdims=True
        )
        query_grad = jnp.zeros((TILE, TILE), F32)
        for t in range(count):
            score = work_ref[t]
            prob = jnp.exp(score - top) * share
            dscore = (prob * (dot(upstream, reads[t](heads + head), NT) - delta)).astype(BF16)
            query_grad = query_grad + dot(dscore, norm_ref[t], NN)
            term = dscore.astype(F32) * score
            query_terms = query_terms + term
            term = jnp.sum(term, axis=0, keepdims=True)
            if head:
                term = term + stat_ref[8 + t : 9 + t, :]
            stat_ref[8 + t : 9 + t, :] = term
        dq_ref[head] = query_grad * scale
        stats = jnp.where(lane == head, level, stats)
        stats = jnp.where(lane == heads + head, delta, stats)
    query_total = jnp.sum(query_terms, axis=1, keepdims=True)
    stats = jnp.where(lane == 2 * heads + 1, query_total, stats)
    rows = jnp.transpose(stats)[0:8]
    place = lax.broadcasted_iota(jnp.int32, (8, TILE), 0)
    stat_ref[0:8, :] = jnp.where(place == 2 * heads, inverse[count : count + 1], rows)
    stat_ref[8 + count : 9 + count, :] = rows[2 * heads + 1 : 2 * heads + 2]
    stat_ref[9 + count :, :] = jnp.zeros((24 - 9 - count, TILE), F32)


def lanes_kernel(heads, near, line, stats_ref, near_ref, far_ref, terms_ref, total_ref):
    count = len(OFFSETS)
    lane = lax.axis_index("y") * lax.axis_size("c") + lax.axis_index("c")
    frame = own_frame()
    half = line * lax.axis_size("x") // 2
    groups = stats_ref.shape[0]
    total = stats_ref[0]
    for group in range(1, groups):
        total = total + stats_ref[group]
    total_ref[...] = total
    last = 2 * heads + 1
    far = jnp.where(lane < 2, near + lane, jnp.where(frame < half, near + 3, near + 2))
    for ref, slot in ((near_ref, 1 + lane), (far_ref, far)):
        term = total_ref[pl.ds(8 + slot, 1), :]
        for group in range(groups):
            ref[group] = stats_ref[group, 0:8]
            ref[group, last : last + 1, :] = term
    terms_ref[0:1, :] = total[8 + count : 9 + count]
    terms_ref[1:2, :] = total[8:9]
    terms_ref[2:, :] = jnp.zeros((6, TILE), F32)


def backward_kernel(
    heads, near, line, channels, sums_ref, terms_ref, own_ref, got_ref,
    q_ref, k_ref, kn_ref, v_ref, dq_ref, gain_ref, gathered_ref, *refs
):
    count = len(OFFSETS)
    tiles = refs[:near]
    gq_ref, gk_ref, dv_ref = refs[near:]
    scale = TILE ** (-0.5)
    inverse_at, term_at = 2 * heads, 2 * heads + 1

    def stat(t, row):
        if t == 0:
            return own_ref[row : row + 1]
        if t < near:
            return got_ref[(t - 1) ^ 1, row : row + 1]
        lane = {0: 1, 1: 0, 2: 2, 3: 2}[t - near]
        return got_ref[lane, 8 + row : 9 + row]

    inverse = lax.rsqrt(sums_ref[...] / channels + EPS)
    squared = inverse * inverse / channels
    key_term = terms_ref[1:2]
    for t in range(1, count):
        if t != count - 1:
            key_term = key_term + stat(t, term_at)
    turned = columns(
        jnp.concatenate(
            [stat(t, inverse_at) for t in range(count)]
            + [
                inverse[0:1],
                squared[count : count + 1] * terms_ref[0:1],
                squared[0:1] * key_term,
            ],
            axis=0,
        )
    )
    frame = own_frame()
    usable = [inside(frame, line, t) for t in range(count)]
    reads = [
        tile_of(tiles, gathered_ref, frame, near, line, t, 2 * heads) for t in range(count)
    ]
    for head in range(heads):
        key, value = kn_ref[head], v_ref[head]
        key_grad = jnp.zeros((TILE, TILE), F32)
        value_grad = jnp.zeros((TILE, TILE), F32)
        for t in range(count):
            query = (
                reads[t](head).astype(F32) * turned[:, t : t + 1] * gain_ref[head : head + 1]
            ).astype(BF16)
            upstream = reads[t](heads + head)
            score = dot(key, query, NT) * scale - stat(t, head)
            prob = jnp.exp(jnp.where(usable[t], score, -1e30))
            value_grad = value_grad + dot(prob.astype(BF16), upstream, NN)
            dprob = dot(value, upstream, NT)
            dscore = prob * (dprob - stat(t, heads + head))
            key_grad = key_grad + dot(dscore.astype(BF16), query, NN)
        dv_ref[head] = value_grad.astype(BF16)
        gk_ref[head] = (
            turned[:, count : count + 1] * (gain_ref[heads + head : heads + head + 1] * (key_grad * scale))
            - k_ref[head].astype(F32) * turned[:, count + 2 : count + 3]
        ).astype(BF16)
        gq_ref[head] = (
            turned[:, 0:1] * (gain_ref[head : head + 1] * dq_ref[head])
            - q_ref[head].astype(F32) * turned[:, count + 1 : count + 2]
        ).astype(BF16)


SEQ, HEAD = ("x", "z"), ("y", "c")


def passed(value, steps, count):
    pairs = [(i, i + steps) for i in range(count) if 0 <= i + steps < count]
    return lax.ppermute(value, SEQ, pairs)


def spread(value, count, line, after=None):
    got = {0: value}
    distance = 1
    while distance < line:
        near = distance // 2
        sources = [got[-near], got[near]]
        if after and distance in after:
            sources = lax.optimization_barrier((*sources, *after[distance]))[:2]
        for facing, source in zip((-1, 1), sources):
            got[facing * distance] = passed(source, -facing * (distance - near), count)
        distance *= 2
    return [got[offset] for offset in OFFSETS if offset in got]


def per_device(total_heads, q_raw, k_raw, values, grad_out, q_gain, k_gain, key_tiles):
    lines, line = lax.axis_size("x"), lax.axis_size("z")
    seq_count = lines * line
    groups = lax.axis_size("y") * lax.axis_size("c")
    heads = q_raw.shape[1]
    channels = float(total_heads * q_raw.shape[2])
    q_raw, k_raw, values, grad_out = [
        jnp.transpose(array, (1, 0, 2)) for array in (q_raw, k_raw, values, grad_out)
    ]
    gains = jnp.concatenate([q_gain, k_gain], axis=0)
    first = jnp.concatenate([k_raw, values], axis=0)
    column = lax.all_gather(
        jnp.concatenate([k_raw, values, q_raw, grad_out], axis=0), "x"
    )
    first_all = spread(first, seq_count, line)
    near = len(first_all)

    vmem = pl.BlockSpec(memory_space=pltpu.VMEM)
    params = pltpu.CompilerParams(vmem_limit_bytes=VMEM_LIMIT)
    whole = (heads, TILE, TILE)
    count = len(OFFSETS)
    sums = pl.pallas_call(
        functools.partial(squares_kernel, heads, near, line),
        out_shape=jax.ShapeDtypeStruct((16, TILE), F32),
        in_specs=[vmem] * (near + 2),
        out_specs=vmem,
        compiler_params=params,
        name="squares",
    )(q_raw, column, *first_all)
    sums = lax.psum(lax.psum(sums, "c"), "y")
    q_late, do_late, *_ = lax.optimization_barrier((q_raw, grad_out, first_all[5], first_all[6]))
    second_all = spread(
        jnp.concatenate([q_late, do_late], axis=0), seq_count, line, {4: (sums,)}
    )
    attended, dq, k_norm, stats = pl.pallas_call(
        functools.partial(forward_kernel, heads, near, line, channels),
        out_shape=[
            jax.ShapeDtypeStruct(whole, BF16),
            jax.ShapeDtypeStruct(whole, F32),
            jax.ShapeDtypeStruct(whole, BF16),
            jax.ShapeDtypeStruct((24, TILE), F32),
        ],
        in_specs=[vmem] * (5 + near),
        out_specs=[vmem] * 4,
        scratch_shapes=[
            pltpu.VMEM((count, TILE, TILE), BF16),
            pltpu.VMEM((count, TILE, TILE), F32),
        ],
        compiler_params=params,
        name="forward",
    )(sums, q_raw, grad_out, gains, column, *first_all)

    stats, *second_all[5:7] = lax.optimization_barrier((stats, *second_all[5:7]))
    gathered = lax.all_gather(lax.all_gather(stats, "c"), "y").reshape(groups, 24, TILE)
    row = jax.ShapeDtypeStruct((groups, 8, TILE), F32)
    near_out, far_out, terms = pl.pallas_call(
        functools.partial(lanes_kernel, heads, near, line),
        out_shape=[row, row, jax.ShapeDtypeStruct((8, TILE), F32)],
        in_specs=[vmem],
        out_specs=[vmem] * 3,
        scratch_shapes=[pltpu.VMEM((24, TILE), F32)],
        compiler_params=params,
        name="lanes",
    )(gathered)
    near_pairs = [
        (frame * groups + at, (frame + OFFSETS[1 + at]) * groups + at)
        for frame in range(seq_count)
        for at in range(near - 1)
        if 0 <= frame + OFFSETS[1 + at] < seq_count
    ]
    far_pairs = [
        (frame * groups + at, (frame + shift) % seq_count * groups + at)
        for frame in range(seq_count)
        for at, shift in enumerate((-line, line, seq_count // 2))
        if at == 2 or 0 <= frame + shift < seq_count
    ]
    near_in = lax.ppermute(near_out, SEQ + HEAD, near_pairs)
    far_in = lax.ppermute(far_out, SEQ + HEAD, far_pairs)
    got = lax.all_to_all(
        jnp.concatenate([near_in, far_in], axis=1), HEAD, 0, 0, tiled=True
    )
    grad_q, grad_k, grad_v = pl.pallas_call(
        functools.partial(backward_kernel, heads, near, line, channels),
        out_shape=[jax.ShapeDtypeStruct(whole, BF16)] * 3,
        in_specs=[vmem] * (11 + near),
        out_specs=[vmem] * 3,
        compiler_params=params,
        name="backward",
    )(
        sums, terms, stats, got, q_raw, k_raw, k_norm, values, dq, gains, column, *second_all,
    )
    return tuple(
        jnp.transpose(array, (1, 0, 2)) for array in (attended, grad_q, grad_k, grad_v)
    )


def solution(mesh):
    split = Mesh(mesh.devices.reshape(4, -1, mesh.shape["head"] // 2, 2), SEQ + HEAD)

    def whole(q_raw, k_raw, values, grad_out, q_gain, k_gain, key_tiles):
        tokens = P(SEQ, HEAD, None)
        return jax.shard_map(
            functools.partial(per_device, q_raw.shape[1]),
            mesh=split,
            in_specs=(tokens,) * 4 + (P(HEAD, None), P(HEAD, None), P()),
            out_specs=(tokens,) * 4,
            check_vma=False,
        )(q_raw, k_raw, values, grad_out, q_gain, k_gain, key_tiles)

    return whole
```

```python
import functools

import jax
import jax.numpy as jnp
from jax import lax
from jax.experimental import pallas as pl
from jax.experimental.pallas import tpu as pltpu
from jax.sharding import Mesh, PartitionSpec as P

TILE = 128
EPS = 1e-06
OFFSETS = (0, -1, 1, -2, 2, -4, 4, -8, 8, -16, 16, -32, 32)
NT = (((1,), (1,)), ((), ()))
NN = (((1,), (0,)), ((), ()))
F32 = jnp.float32
BF16 = jnp.bfloat16
VMEM_LIMIT = 48 * 1024 * 1024


def dot(left, right, dims):
    return lax.dot_general(left, right, dims, preferred_element_type=F32)


def row_sums(square):
    ones = jnp.ones((8, TILE), BF16)
    high = square.astype(BF16)
    low = (square - high.astype(F32)).astype(BF16)
    return dot(ones, high, NT) + dot(ones, low, NT)


def columns(rows):
    fill = jnp.zeros((TILE - rows.shape[0], TILE), F32)
    return jnp.transpose(jnp.concatenate([rows, fill], axis=0))


def own_frame():
    return lax.axis_index("x") * lax.axis_size("z") + lax.axis_index("z")


def mirrored(value):
    return value * (1 - 2 * lax.axis_index("c"))


def shared_place(place):
    return 1 + ((place - 1) ^ lax.axis_index("c")) if place else 0


def inside(frame, line, place):
    at = frame + mirrored(OFFSETS[place])
    return (at >= 0) & (at < line * lax.axis_size("x"))


def tile_of(tiles, gathered_ref, frame, near, line, place, skip=0):
    if place < near:
        return lambda i: tiles[place][i]
    at = frame // line + mirrored(OFFSETS[place] // line)
    at = jnp.minimum(jnp.maximum(at, 0), gathered_ref.shape[0] - 1)
    return lambda i: gathered_ref[at, skip + i]


def squares_kernel(heads, near, line, q_ref, gathered_ref, *refs):
    tiles, out_ref = refs[:-1], refs[-1]
    count = len(OFFSETS)
    frame = own_frame()
    reads = [tile_of(tiles, gathered_ref, frame, near, line, t) for t in range(count)]
    reads.append(lambda i: q_ref[i])
    for place, read in enumerate(reads):
        total = jnp.zeros((TILE, TILE), F32)
        for head in range(heads):
            floats = read(head).astype(F32)
            total = total + floats * floats
        row = shared_place(place) if place < count else place
        out_ref[pl.ds(row, 1), :] = row_sums(total)[0:1]
    out_ref[count + 1 :, :] = jnp.zeros((16 - count - 1, TILE), F32)


def forward_kernel(
    heads, near, line, channels, sums_ref, q_ref, do_ref, gain_ref, gathered_ref, *refs
):
    count = len(OFFSETS)
    tiles = refs[:near]
    out_ref, dq_ref, kn_ref, stat_ref, norm_ref, work_ref = refs[near:]
    scale = TILE ** (-0.5)
    places = [shared_place(t) for t in range(count)] + [count]
    sums = jnp.concatenate([sums_ref[pl.ds(place, 1), :] for place in places], axis=0)
    inverse = lax.rsqrt(sums / channels + EPS)
    turned = columns(inverse)
    frame = own_frame()
    usable = [inside(frame, line, t) for t in range(count)]
    reads = [tile_of(tiles, gathered_ref, frame, near, line, t) for t in range(count)]
    lane = lax.broadcasted_iota(jnp.int32, (TILE, TILE), 1)
    stats = jnp.zeros((TILE, TILE), F32)
    query_terms = jnp.zeros((TILE, TILE), F32)
    for head in range(heads):
        query = (
            q_ref[head].astype(F32) * turned[:, count : count + 1] * gain_ref[head : head + 1]
        ).astype(BF16)
        upstream = do_ref[head]
        top = jnp.full((TILE, TILE), -1e30, F32)
        for t in range(count):
            key = (
                reads[t](head).astype(F32) * turned[:, t : t + 1] * gain_ref[heads + head : heads + head + 1]
            ).astype(BF16)
            norm_ref[t] = key
            if t == 0:
                kn_ref[head] = key
            score = dot(query, key, NT) * scale
            score = jnp.where(usable[t], score, -1e30)
            work_ref[t] = score
            top = jnp.maximum(top, score)
        top = jnp.max(top, axis=1, keepdims=True)
        total = jnp.zeros((TILE, TILE), F32)
        for t in range(count):
            total = total + jnp.exp(work_ref[t] - top)
        total = jnp.sum(total, axis=1, keepdims=True)
        level = top + jnp.log(total)
        share = 1.0 / total
        out = jnp.zeros((TILE, TILE), F32)
        for t in range(count):
            prob = jnp.exp(work_ref[t] - top) * share
            out = out + dot(prob.astype(BF16), reads[t](heads + head), NN)
        out = out.astype(BF16)
        out_ref[head] = out
        delta = jnp.sum(
            upstream.astype(F32) * out.astype(F32), axis=1, keepdims=True
        )
        query_grad = jnp.zeros((TILE, TILE), F32)
        for t in range(count):
            score = work_ref[t]
            prob = jnp.exp(score - top) * share
            dscore = (prob * (dot(upstream, reads[t](heads + head), NT) - delta)).astype(BF16)
            query_grad = query_grad + dot(dscore, norm_ref[t], NN)
            term = dscore.astype(F32) * score
            query_terms = query_terms + term
            term = jnp.sum(term, axis=0, keepdims=True)
            row = pl.ds(8 + places[t], 1)
            if head:
                term = term + stat_ref[row, :]
            stat_ref[row, :] = term
        dq_ref[head] = query_grad * scale
        stats = jnp.where(lane == head, level, stats)
        stats = jnp.where(lane == heads + head, delta, stats)
    query_total = jnp.sum(query_terms, axis=1, keepdims=True)
    stats = jnp.where(lane == 2 * heads + 1, query_total, stats)
    rows = jnp.transpose(stats)[0:8]
    place = lax.broadcasted_iota(jnp.int32, (8, TILE), 0)
    stat_ref[0:8, :] = jnp.where(place == 2 * heads, inverse[count : count + 1], rows)
    stat_ref[8 + count : 9 + count, :] = rows[2 * heads + 1 : 2 * heads + 2]
    stat_ref[9 + count :, :] = jnp.zeros((24 - 9 - count, TILE), F32)


def lanes_kernel(heads, near, line, stats_ref, near_ref, far_ref, terms_ref, total_ref):
    count = len(OFFSETS)
    lane = lax.axis_index("y") * lax.axis_size("c") + lax.axis_index("c")
    frame = own_frame()
    half = line * lax.axis_size("x") // 2
    groups = stats_ref.shape[0]
    total = stats_ref[0]
    for group in range(1, groups):
        total = total + stats_ref[group]
    total_ref[...] = total
    last = 2 * heads + 1
    far = jnp.where(lane < 2, near + lane, jnp.where(frame < half, near + 3, near + 2))
    for ref, slot in ((near_ref, 1 + lane), (far_ref, far)):
        term = total_ref[pl.ds(8 + slot, 1), :]
        for group in range(groups):
            ref[group] = stats_ref[group, 0:8]
            ref[group, last : last + 1, :] = term
    terms_ref[0:1, :] = total[8 + count : 9 + count]
    terms_ref[1:2, :] = total[8:9]
    terms_ref[2:, :] = jnp.zeros((6, TILE), F32)


def backward_kernel(
    heads, near, line, channels, sums_ref, terms_ref, own_ref, got_ref,
    q_ref, k_ref, kn_ref, v_ref, dq_ref, gain_ref, gathered_ref, *refs
):
    count = len(OFFSETS)
    tiles = refs[:near]
    gq_ref, gk_ref, dv_ref = refs[near:]
    scale = TILE ** (-0.5)
    inverse_at, term_at = 2 * heads, 2 * heads + 1
    core = lax.axis_index("c")

    def stat(t, row):
        if t == 0:
            return own_ref[row : row + 1]
        if t < near:
            return got_ref[(t - 1) ^ 1 ^ core, row : row + 1]
        lane = (t - near) ^ 1 ^ core if t - near < 2 else 2
        return got_ref[lane, 8 + row : 9 + row]

    inverse = lax.rsqrt(sums_ref[...] / channels + EPS)
    squared = inverse * inverse / channels
    key_term = terms_ref[1:2]
    for t in range(1, count):
        if t != count - 1:
            key_term = key_term + stat(t, term_at)
    turned = columns(
        jnp.concatenate(
            [stat(t, inverse_at) for t in range(count)]
            + [
                inverse[0:1],
                squared[count : count + 1] * terms_ref[0:1],
                squared[0:1] * key_term,
            ],
            axis=0,
        )
    )
    frame = own_frame()
    usable = [inside(frame, line, t) for t in range(count)]
    reads = [
        tile_of(tiles, gathered_ref, frame, near, line, t, 2 * heads) for t in range(count)
    ]
    for head in range(heads):
        key, value = kn_ref[head], v_ref[head]
        key_grad = jnp.zeros((TILE, TILE), F32)
        value_grad = jnp.zeros((TILE, TILE), F32)
        for t in range(count):
            query = (
                reads[t](head).astype(F32) * turned[:, t : t + 1] * gain_ref[head : head + 1]
            ).astype(BF16)
            upstream = reads[t](heads + head)
            score = dot(key, query, NT) * scale - stat(t, head)
            prob = jnp.exp(jnp.where(usable[t], score, -1e30))
            value_grad = value_grad + dot(prob.astype(BF16), upstream, NN)
            dprob = dot(value, upstream, NT)
            dscore = prob * (dprob - stat(t, heads + head))
            key_grad = key_grad + dot(dscore.astype(BF16), query, NN)
        dv_ref[head] = value_grad.astype(BF16)
        gk_ref[head] = (
            turned[:, count : count + 1] * (gain_ref[heads + head : heads + head + 1] * (key_grad * scale))
            - k_ref[head].astype(F32) * turned[:, count + 2 : count + 3]
        ).astype(BF16)
        gq_ref[head] = (
            turned[:, 0:1] * (gain_ref[head : head + 1] * dq_ref[head])
            - q_ref[head].astype(F32) * turned[:, count + 1 : count + 2]
        ).astype(BF16)


SEQ, HEAD = ("x", "z"), ("y", "c")


def passed(value, steps, count):
    pairs = [
        (2 * i + core, 2 * (i + way * steps) + core)
        for i in range(count)
        for core, way in enumerate((1, -1))
        if 0 <= i + way * steps < count
    ]
    return lax.ppermute(value, SEQ + ("c",), pairs)


def spread(value, count, line, after=None):
    got = {0: value}
    distance = 1
    while distance < line:
        near = distance // 2
        sources = [got[-near], got[near]]
        if after and distance in after:
            sources = lax.optimization_barrier((*sources, *after[distance]))[:2]
        for facing, source in zip((-1, 1), sources):
            got[facing * distance] = passed(source, -facing * (distance - near), count)
        distance *= 2
    return [got[offset] for offset in OFFSETS if offset in got]


def per_device(total_heads, q_raw, k_raw, values, grad_out, q_gain, k_gain, key_tiles):
    lines, line = lax.axis_size("x"), lax.axis_size("z")
    seq_count = lines * line
    groups = lax.axis_size("y") * lax.axis_size("c")
    heads = q_raw.shape[1]
    channels = float(total_heads * q_raw.shape[2])
    q_raw, k_raw, values, grad_out = [
        jnp.transpose(array, (1, 0, 2)) for array in (q_raw, k_raw, values, grad_out)
    ]
    gains = jnp.concatenate([q_gain, k_gain], axis=0)
    first = jnp.concatenate([k_raw, values], axis=0)
    column = lax.all_gather(
        jnp.concatenate([k_raw, values, q_raw, grad_out], axis=0), "x"
    )
    first_all = spread(first, seq_count, line)
    near = len(first_all)

    vmem = pl.BlockSpec(memory_space=pltpu.VMEM)
    params = pltpu.CompilerParams(vmem_limit_bytes=VMEM_LIMIT)
    whole = (heads, TILE, TILE)
    count = len(OFFSETS)
    sums = pl.pallas_call(
        functools.partial(squares_kernel, heads, near, line),
        out_shape=jax.ShapeDtypeStruct((16, TILE), F32),
        in_specs=[vmem] * (near + 2),
        out_specs=vmem,
        compiler_params=params,
        name="squares",
    )(q_raw, column, *first_all)
    sums = lax.psum(lax.psum(sums, "c"), "y")
    attended, dq, k_norm, stats = pl.pallas_call(
        functools.partial(forward_kernel, heads, near, line, channels),
        out_shape=[
            jax.ShapeDtypeStruct(whole, BF16),
            jax.ShapeDtypeStruct(whole, F32),
            jax.ShapeDtypeStruct(whole, BF16),
            jax.ShapeDtypeStruct((24, TILE), F32),
        ],
        in_specs=[vmem] * (5 + near),
        out_specs=[vmem] * 4,
        scratch_shapes=[
            pltpu.VMEM((count, TILE, TILE), BF16),
            pltpu.VMEM((count, TILE, TILE), F32),
        ],
        compiler_params=params,
        name="forward",
    )(sums, q_raw, grad_out, gains, column, *first_all)

    q_late, do_late, *_ = lax.optimization_barrier((q_raw, grad_out, *first_all[-4:-2]))
    second_all = spread(
        jnp.concatenate([q_late, do_late], axis=0), seq_count, line, {2: (sums,), 4: (attended,)}
    )
    stats, *second_all[-4:-2] = lax.optimization_barrier((stats, *second_all[-4:-2]))
    gathered = lax.all_gather(lax.all_gather(stats, "c"), "y").reshape(groups, 24, TILE)
    row = jax.ShapeDtypeStruct((groups, 8, TILE), F32)
    near_out, far_out, terms = pl.pallas_call(
        functools.partial(lanes_kernel, heads, near, line),
        out_shape=[row, row, jax.ShapeDtypeStruct((8, TILE), F32)],
        in_specs=[vmem],
        out_specs=[vmem] * 3,
        scratch_shapes=[pltpu.VMEM((24, TILE), F32)],
        compiler_params=params,
        name="lanes",
    )(gathered)
    near_pairs = [
        (frame * groups + at, (frame + OFFSETS[1 + at]) * groups + at)
        for frame in range(seq_count)
        for at in range(near - 1)
        if 0 <= frame + OFFSETS[1 + at] < seq_count
    ]
    far_pairs = [
        (frame * groups + at, (frame + shift) % seq_count * groups + at)
        for frame in range(seq_count)
        for at, shift in enumerate((-line, line, seq_count // 2))
        if at == 2 or 0 <= frame + shift < seq_count
    ]
    near_in = lax.ppermute(near_out, SEQ + HEAD, near_pairs)
    far_in = lax.ppermute(far_out, SEQ + HEAD, far_pairs)
    got = lax.all_to_all(
        jnp.concatenate([near_in, far_in], axis=1), HEAD, 0, 0, tiled=True
    )
    grad_q, grad_k, grad_v = pl.pallas_call(
        functools.partial(backward_kernel, heads, near, line, channels),
        out_shape=[jax.ShapeDtypeStruct(whole, BF16)] * 3,
        in_specs=[vmem] * (11 + near),
        out_specs=[vmem] * 3,
        compiler_params=params,
        name="backward",
    )(
        sums, terms, stats, got, q_raw, k_raw, k_norm, values, dq, gains, column, *second_all,
    )
    return tuple(
        jnp.transpose(array, (1, 0, 2)) for array in (attended, grad_q, grad_k, grad_v)
    )


def solution(mesh):
    split = Mesh(mesh.devices.reshape(4, -1, mesh.shape["head"] // 2, 2), SEQ + HEAD)

    def whole(q_raw, k_raw, values, grad_out, q_gain, k_gain, key_tiles):
        tokens = P(SEQ, HEAD, None)
        return jax.shard_map(
            functools.partial(per_device, q_raw.shape[1]),
            mesh=split,
            in_specs=(tokens,) * 4 + (P(HEAD, None), P(HEAD, None), P()),
            out_specs=(tokens,) * 4,
            check_vma=False,
        )(q_raw, k_raw, values, grad_out, q_gain, k_gain, key_tiles)

    return whole
```

```python
import functools

import jax
import jax.numpy as jnp
from jax import lax
from jax.experimental import pallas as pl
from jax.experimental.pallas import tpu as pltpu
from jax.sharding import Mesh, PartitionSpec as P

TILE = 128
EPS = 1e-06
NEAR = (0, -1, 1, -2, 2, -4, 4, -8, 8)
FAR = 3
NT = (((1,), (1,)), ((), ()))
NN = (((1,), (0,)), ((), ()))
TN = (((0,), (0,)), ((), ()))
F32 = jnp.float32
BF16 = jnp.bfloat16
VMEM_LIMIT = 48 * 1024 * 1024


def dot(left, right, dims):
    return lax.dot_general(left, right, dims, preferred_element_type=F32)


def row_sums(square):
    ones = jnp.ones((8, TILE), BF16)
    high = square.astype(BF16)
    low = (square - high.astype(F32)).astype(BF16)
    return dot(ones, high, NT) + dot(ones, low, NT)


def columns(rows):
    fill = jnp.zeros((TILE - rows.shape[0], TILE), F32)
    return jnp.transpose(jnp.concatenate([rows, fill], axis=0))


def own_frame():
    return lax.axis_index("x") * lax.axis_size("z") + lax.axis_index("z")


def mirrored(value):
    return value * (1 - 2 * lax.axis_index("c"))


def shared_place(place):
    if place == 0 or place == len(NEAR) + FAR - 1:
        return place
    return 1 + ((place - 1) ^ lax.axis_index("c"))


def inside(place):
    line, lines = lax.axis_size("z"), lax.axis_size("x")
    near = len(NEAR)
    if place == 0 or place == near + FAR - 1:
        return None
    offset = NEAR[place] if place < near else (-line, line)[place - near]
    at = own_frame() + mirrored(offset)
    return (at >= 0) & (at < line * lines)


def reader(tiles, gathered_ref, place):
    if place < len(NEAR):
        return lambda i: tiles[place][i]
    lines = lax.axis_size("x")
    step = (mirrored(-1), mirrored(1), lines // 2)[place - len(NEAR)]
    at = lax.rem(lax.axis_index("x") + step + lines, lines)
    return lambda i: gathered_ref[at, i]


def squares_kernel(heads, q_ref, gathered_ref, *refs):
    tiles, out_ref = refs[:-1], refs[-1]
    count = len(NEAR) + FAR
    out_ref[...] = jnp.zeros(out_ref.shape, F32)
    for place in range(count + 1):
        if len(tiles) <= place < len(NEAR):
            continue
        read = reader(tiles, gathered_ref, place) if place < count else lambda i: q_ref[i]
        total = jnp.zeros((TILE, TILE), F32)
        for head in range(heads):
            floats = read(head).astype(F32)
            total = total + floats * floats
        row = shared_place(place) if place < count else place
        out_ref[pl.ds(row, 1), :] = row_sums(total)[0:1]


def attention_kernel(
    heads, channels, sums_ref, before_ref, after_ref, q_ref, do_ref, gain_ref, gathered_ref, *refs
):
    near = len(NEAR)
    count = near + FAR
    tiles = refs[:near]
    out_ref, dq_ref = refs[near : near + 2]
    part_refs = refs[near + 2 : -2]
    norm_ref, work_ref = refs[-2:]
    scale = TILE ** (-0.5)
    rows = []
    for place in range(count):
        if near - 2 <= place < near:
            ref = (before_ref, after_ref)[place - near + 2]
            rows.append(ref[pl.ds(shared_place(place - 2), 1), :])
        else:
            rows.append(sums_ref[pl.ds(shared_place(place), 1), :])
    rows.append(sums_ref[count : count + 1, :])
    turned = columns(lax.rsqrt(jnp.concatenate(rows, axis=0) / channels + EPS))
    usable = [inside(t) for t in range(count)]
    reads = [reader(tiles, gathered_ref, t) for t in range(count)]
    for head in range(heads):
        query = (
            q_ref[head].astype(F32) * turned[:, count : count + 1] * gain_ref[head : head + 1]
        ).astype(BF16)
        upstream = do_ref[head]
        top = jnp.full((TILE, TILE), -1e30, F32)
        for t in range(count):
            key = (
                reads[t](head).astype(F32)
                * turned[:, t : t + 1]
                * gain_ref[heads + head : heads + head + 1]
            ).astype(BF16)
            norm_ref[t] = key
            score = dot(query, key, NT) * scale
            if usable[t] is not None:
                score = jnp.where(usable[t], score, -1e30)
            work_ref[t] = score
            top = jnp.maximum(top, score)
        top = jnp.max(top, axis=1, keepdims=True)
        total = jnp.zeros((TILE, TILE), F32)
        for t in range(count):
            weight = jnp.exp(work_ref[t] - top)
            work_ref[t] = weight
            total = total + weight
        share = 1.0 / jnp.sum(total, axis=1, keepdims=True)
        out = jnp.zeros((TILE, TILE), F32)
        for t in range(count):
            prob = (work_ref[t] * share).astype(BF16)
            out = out + dot(prob, reads[t](heads + head), NN)
            part = part_refs[t]
            part[heads + head] = dot(prob, upstream, TN).astype(part.dtype)
        out = out.astype(BF16)
        out_ref[head] = out
        delta = jnp.sum(upstream.astype(F32) * out.astype(F32), axis=1, keepdims=True)
        query_grad = jnp.zeros((TILE, TILE), F32)
        for t in range(count):
            prob = work_ref[t] * share
            dscore = (prob * (dot(upstream, reads[t](heads + head), NT) - delta)).astype(BF16)
            query_grad = query_grad + dot(dscore, norm_ref[t], NN)
            part = part_refs[t]
            part[head] = (dot(dscore, query, TN) * scale).astype(part.dtype)
        dq_ref[head] = query_grad * scale


def terms_kernel(heads, q_ref, k_ref, dq_ref, gain_ref, *refs):
    parts, (dk_ref, dv_ref, terms_ref) = refs[:-3], refs[-3:]
    query_total = jnp.zeros((TILE, TILE), F32)
    key_total = jnp.zeros((TILE, TILE), F32)
    for head in range(heads):
        key_grad, value_grad = parts[0][head], parts[0][heads + head]
        for part in parts[1:]:
            key_grad = key_grad + part[head].astype(F32)
            value_grad = value_grad + part[heads + head].astype(F32)
        dk_ref[head] = key_grad
        dv_ref[head] = value_grad.astype(BF16)
        query_total = query_total + q_ref[head].astype(F32) * (
            dq_ref[head] * gain_ref[head : head + 1]
        )
        key_total = key_total + k_ref[head].astype(F32) * (
            key_grad * gain_ref[heads + head : heads + head + 1]
        )
    terms_ref[...] = jnp.zeros(terms_ref.shape, F32)
    terms_ref[0:1, :] = row_sums(query_total)[0:1]
    terms_ref[1:2, :] = row_sums(key_total)[0:1]


def final_kernel(
    heads, channels, sums_ref, terms_ref, q_ref, k_ref, dq_ref, dk_ref, gain_ref, gq_ref, gk_ref
):
    count = len(NEAR) + FAR
    inverse = lax.rsqrt(
        jnp.concatenate([sums_ref[count : count + 1], sums_ref[0:1]], axis=0) / channels + EPS
    )
    cubes = inverse * inverse * inverse * terms_ref[0:2] / channels
    turned = columns(jnp.concatenate([inverse, cubes], axis=0))
    for head in range(heads):
        gq_ref[head] = (
            turned[:, 0:1] * (gain_ref[head : head + 1] * dq_ref[head])
            - q_ref[head].astype(F32) * turned[:, 2:3]
        ).astype(BF16)
        gk_ref[head] = (
            turned[:, 1:2] * (gain_ref[heads + head : heads + head + 1] * dk_ref[head])
            - k_ref[head].astype(F32) * turned[:, 3:4]
        ).astype(BF16)


SEQ, HEAD = ("x", "z"), ("y", "c")


def passed(value, steps):
    count = lax.axis_size("x") * lax.axis_size("z")
    pairs = [
        (2 * i + core, 2 * (i + way * steps) + core)
        for i in range(count)
        for core, way in enumerate((1, -1))
        if 0 <= i + way * steps < count
    ]
    return lax.ppermute(value, SEQ + ("c",), pairs)


def spread(value):
    got = {0: value}
    for offset in NEAR[1:]:
        half = abs(offset) // 2 * (1 if offset > 0 else -1)
        got[offset] = passed(got[half], half - offset)
    return [got[offset] for offset in NEAR]


def collect(parts):
    arrived = []
    for side in (1, 2):
        carried = parts[len(NEAR) - 3 + side]
        for place in range(len(NEAR) - 3 + side, 0, -2):
            offset = NEAR[place]
            half = abs(offset) // 2 * (1 if offset > 0 else -1)
            carried = passed(carried, offset - half)
            if half:
                carried = (carried.astype(F32) + parts[place - 2]).astype(BF16)
        arrived.append(carried)
    return arrived


def per_device(total_heads, q_raw, k_raw, values, grad_out, q_gain, k_gain, key_tiles):
    lines, line = lax.axis_size("x"), lax.axis_size("z")
    seq_count = lines * line
    near = len(NEAR)
    count = near + FAR
    heads = q_raw.shape[1]
    channels = float(total_heads * q_raw.shape[2])
    q_raw, k_raw, values, grad_out = [
        jnp.transpose(array, (1, 0, 2)) for array in (q_raw, k_raw, values, grad_out)
    ]
    gains = jnp.concatenate([q_gain, k_gain], axis=0)
    first = jnp.concatenate([k_raw, values], axis=0)
    column = lax.all_gather(jnp.concatenate([first, jnp.zeros_like(k_raw[:2])], axis=0), "x")
    tiles = spread(first)

    vmem = pl.BlockSpec(memory_space=pltpu.VMEM)
    params = pltpu.CompilerParams(vmem_limit_bytes=VMEM_LIMIT)
    whole, pair = (heads, TILE, TILE), (2 * heads, TILE, TILE)
    sums = pl.pallas_call(
        functools.partial(squares_kernel, heads),
        out_shape=jax.ShapeDtypeStruct((16, TILE), F32),
        in_specs=[vmem] * near,
        out_specs=vmem,
        compiler_params=params,
        name="squares",
    )(q_raw, column, *tiles[: near - 2])
    sums = lax.psum(lax.psum(sums, "c"), "y")
    reach = NEAR[near - 3]
    before, after = passed(sums, reach), passed(sums, -reach)
    attended, dq, *parts = pl.pallas_call(
        functools.partial(attention_kernel, heads, channels),
        out_shape=[jax.ShapeDtypeStruct(whole, BF16), jax.ShapeDtypeStruct(whole, F32)]
        + [jax.ShapeDtypeStruct(pair, F32 if t < near - 2 else BF16) for t in range(count)],
        in_specs=[vmem] * (7 + near),
        out_specs=[vmem] * (2 + count),
        scratch_shapes=[
            pltpu.VMEM((count, TILE, TILE), BF16),
            pltpu.VMEM((count, TILE, TILE), F32),
        ],
        compiler_params=params,
        name="attention",
    )(sums, before, after, q_raw, grad_out, gains, column, *tiles)
    arrived = collect(parts) + [passed(parts[near], -line), passed(parts[near + 1], line)]
    arrived.append(
        lax.ppermute(
            parts[near + 2], SEQ, [(i, (i + seq_count // 2) % seq_count) for i in range(seq_count)]
        )
    )
    dk, grad_v, terms = pl.pallas_call(
        functools.partial(terms_kernel, heads),
        out_shape=[
            jax.ShapeDtypeStruct(whole, F32),
            jax.ShapeDtypeStruct(whole, BF16),
            jax.ShapeDtypeStruct((8, TILE), F32),
        ],
        in_specs=[vmem] * (5 + len(arrived)),
        out_specs=[vmem] * 3,
        compiler_params=params,
        name="terms",
    )(q_raw, k_raw, dq, gains, parts[0], *arrived)
    terms = lax.psum(lax.psum(terms, "c"), "y")
    grad_q, grad_k = pl.pallas_call(
        functools.partial(final_kernel, heads, channels),
        out_shape=[jax.ShapeDtypeStruct(whole, BF16)] * 2,
        in_specs=[vmem] * 7,
        out_specs=[vmem] * 2,
        compiler_params=params,
        name="final",
    )(sums, terms, q_raw, k_raw, dq, dk, gains)
    return tuple(
        jnp.transpose(array, (1, 0, 2)) for array in (attended, grad_q, grad_k, grad_v)
    )


def solution(mesh):
    split = Mesh(mesh.devices.reshape(4, -1, mesh.shape["head"] // 2, 2), SEQ + HEAD)

    def whole(q_raw, k_raw, values, grad_out, q_gain, k_gain, key_tiles):
        tokens = P(SEQ, HEAD, None)
        return jax.shard_map(
            functools.partial(per_device, q_raw.shape[1]),
            mesh=split,
            in_specs=(tokens,) * 4 + (P(HEAD, None), P(HEAD, None), P()),
            out_specs=(tokens,) * 4,
            check_vma=False,
        )(q_raw, k_raw, values, grad_out, q_gain, k_gain, key_tiles)

    return whole
```

```python
import functools

import jax
import jax.numpy as jnp
from jax import lax
from jax.experimental import pallas as pl
from jax.experimental.pallas import tpu as pltpu
from jax.sharding import Mesh, PartitionSpec as P

TILE = 128
EPS = 1e-06
NEAR = (0, -1, 1, -2, 2, -4, 4, -8, 8)
FAR = 3
NT = (((1,), (1,)), ((), ()))
NN = (((1,), (0,)), ((), ()))
TN = (((0,), (0,)), ((), ()))
F32 = jnp.float32
BF16 = jnp.bfloat16
VMEM_LIMIT = 48 * 1024 * 1024


def dot(left, right, dims):
    return lax.dot_general(left, right, dims, preferred_element_type=F32)


def row_sums(square):
    ones = jnp.ones((8, TILE), BF16)
    high = square.astype(BF16)
    low = (square - high.astype(F32)).astype(BF16)
    return dot(ones, high, NT) + dot(ones, low, NT)


def columns(rows):
    fill = jnp.zeros((TILE - rows.shape[0], TILE), F32)
    return jnp.transpose(jnp.concatenate([rows, fill], axis=0))


def own_frame():
    return lax.axis_index("x") * lax.axis_size("z") + lax.axis_index("z")


def mirrored(value):
    return value * (1 - 2 * lax.axis_index("c"))


def inside(place):
    line, lines = lax.axis_size("z"), lax.axis_size("x")
    near = len(NEAR)
    if place == 0 or place == near + FAR - 1:
        return None
    offset = NEAR[place] if place < near else (-line, line)[place - near]
    at = own_frame() + mirrored(offset)
    return (at >= 0) & (at < line * lines)


def squares_kernel(heads, q_ref, k_ref, out_ref):
    out_ref[...] = jnp.zeros(out_ref.shape, F32)
    for row, ref in enumerate((q_ref, k_ref)):
        total = jnp.zeros((TILE, TILE), F32)
        for head in range(heads):
            floats = ref[head].astype(F32)
            total = total + floats * floats
        total = row_sums(total)[0:1]
        for group in range(out_ref.shape[0]):
            out_ref[group, row : row + 1, :] = total


def group_sum(ref):
    total = ref[0]
    for group in range(1, ref.shape[0]):
        total = total + ref[group]
    return total


def norm_kernel(heads, channels, sums_ref, q_ref, k_ref, v_ref, gain_ref, qn_ref, kv_ref, inverse_ref):
    inverse = lax.rsqrt(group_sum(sums_ref) / channels + EPS)
    inverse_ref[...] = inverse
    turned = columns(inverse)
    for head in range(heads):
        qn_ref[head] = (
            q_ref[head].astype(F32) * turned[:, 0:1] * gain_ref[head : head + 1]
        ).astype(BF16)
        kv_ref[head] = (
            k_ref[head].astype(F32) * turned[:, 1:2] * gain_ref[heads + head : heads + head + 1]
        ).astype(BF16)
        kv_ref[heads + head] = v_ref[head]


def attention_kernel(heads, q_ref, do_ref, *refs):
    count = len(NEAR) + FAR
    tiles = refs[:count]
    out_ref, dq_ref = refs[count : count + 2]
    part_refs = refs[count + 2 : -1]
    work_ref = refs[-1]
    scale = TILE ** (-0.5)
    usable = [inside(t) for t in range(count)]
    tops, shares, deltas = [], [], []
    for head in range(heads):
        top = jnp.full((TILE, TILE), -1e30, F32)
        for t in range(count):
            score = dot(q_ref[head], tiles[t][head], NT) * scale
            if usable[t] is not None:
                score = jnp.where(usable[t], score, -1e30)
            work_ref[head, t] = score
            top = jnp.maximum(top, score)
        tops.append(jnp.max(top, axis=1, keepdims=True))
    for head in range(heads):
        total = jnp.zeros((TILE, TILE), F32)
        for t in range(count):
            weight = jnp.exp(work_ref[head, t] - tops[head])
            work_ref[head, t] = weight
            total = total + weight
        shares.append(1.0 / jnp.sum(total, axis=1, keepdims=True))
    for head in range(heads):
        upstream = do_ref[head]
        out = jnp.zeros((TILE, TILE), F32)
        for t in range(count):
            prob = work_ref[head, t] * shares[head]
            work_ref[head, t] = prob
            prob = prob.astype(BF16)
            out = out + dot(prob, tiles[t][heads + head], NN)
            part = part_refs[t]
            part[heads + head] = dot(prob, upstream, TN).astype(part.dtype)
        out = out.astype(BF16)
        out_ref[head] = out
        deltas.append(jnp.sum(upstream.astype(F32) * out.astype(F32), axis=1, keepdims=True))
    for head in range(heads):
        query, upstream = q_ref[head], do_ref[head]
        query_grad = jnp.zeros((TILE, TILE), F32)
        for t in range(count):
            dprob = dot(upstream, tiles[t][heads + head], NT)
            dscore = (work_ref[head, t] * (dprob - deltas[head])).astype(BF16)
            query_grad = query_grad + dot(dscore, tiles[t][head], NN)
            part = part_refs[t]
            part[head] = (dot(dscore, query, TN) * scale).astype(part.dtype)
        dq_ref[head] = query_grad * scale


def terms_kernel(heads, q_ref, k_ref, dq_ref, gain_ref, *refs):
    parts, (dk_ref, dv_ref, terms_ref) = refs[:-3], refs[-3:]
    query_total = jnp.zeros((TILE, TILE), F32)
    key_total = jnp.zeros((TILE, TILE), F32)
    for head in range(heads):
        key_grad, value_grad = parts[0][head], parts[0][heads + head]
        for part in parts[1:]:
            key_grad = key_grad + part[head].astype(F32)
            value_grad = value_grad + part[heads + head].astype(F32)
        dk_ref[head] = key_grad
        dv_ref[head] = value_grad.astype(BF16)
        query_total = query_total + q_ref[head].astype(F32) * (
            dq_ref[head] * gain_ref[head : head + 1]
        )
        key_total = key_total + k_ref[head].astype(F32) * (
            key_grad * gain_ref[heads + head : heads + head + 1]
        )
    terms_ref[...] = jnp.zeros(terms_ref.shape, F32)
    for row, total in enumerate((query_total, key_total)):
        total = row_sums(total)[0:1]
        for group in range(terms_ref.shape[0]):
            terms_ref[group, row : row + 1, :] = total


def final_kernel(
    heads, channels, inverse_ref, terms_ref, q_ref, k_ref, dq_ref, dk_ref, gain_ref, gq_ref, gk_ref
):
    inverse = inverse_ref[0:2]
    cubes = inverse * inverse * inverse * group_sum(terms_ref)[0:2] / channels
    turned = columns(jnp.concatenate([inverse, cubes], axis=0))
    for head in range(heads):
        gq_ref[head] = (
            turned[:, 0:1] * (gain_ref[head : head + 1] * dq_ref[head])
            - q_ref[head].astype(F32) * turned[:, 2:3]
        ).astype(BF16)
        gk_ref[head] = (
            turned[:, 1:2] * (gain_ref[heads + head : heads + head + 1] * dk_ref[head])
            - k_ref[head].astype(F32) * turned[:, 3:4]
        ).astype(BF16)


SEQ, HEAD = ("x", "z"), ("y", "c")


def passed(value, steps):
    count = lax.axis_size("x") * lax.axis_size("z")
    pairs = [
        (2 * i + core, 2 * (i + way * steps) + core)
        for i in range(count)
        for core, way in enumerate((1, -1))
        if 0 <= i + way * steps < count
    ]
    return lax.ppermute(value, SEQ + ("c",), pairs)


def half_round(value):
    count = lax.axis_size("x") * lax.axis_size("z")
    return lax.ppermute(value, SEQ, [(i, (i + count // 2) % count) for i in range(count)])


def relay(offset):
    return int(offset / 2) if abs(offset) > 2 else 0


def spread(value):
    got = {0: value}
    for offset in NEAR[1:]:
        got[offset] = passed(got[relay(offset)], relay(offset) - offset)
    return [got[offset] for offset in NEAR]


def collect(parts):
    arrived = [passed(parts[place], NEAR[place]) for place in (1, 2)]
    for place in (len(NEAR) - 2, len(NEAR) - 1):
        carried = parts[place]
        while place > 2:
            offset = NEAR[place]
            carried = passed(carried, offset - relay(offset))
            place = place - 2
            if relay(offset):
                carried = (carried.astype(F32) + parts[place]).astype(BF16)
            else:
                break
        arrived.append(carried)
    return arrived


def per_device(total_heads, q_raw, k_raw, values, grad_out, q_gain, k_gain, key_tiles):
    line = lax.axis_size("z")
    groups = lax.axis_size("y") * lax.axis_size("c")
    near = len(NEAR)
    count = near + FAR
    heads = q_raw.shape[1]
    channels = float(total_heads * q_raw.shape[2])
    q_raw, k_raw, values, grad_out = [
        jnp.transpose(array, (1, 0, 2)) for array in (q_raw, k_raw, values, grad_out)
    ]
    gains = jnp.concatenate([q_gain, k_gain], axis=0)
    vmem = pl.BlockSpec(memory_space=pltpu.VMEM)
    params = pltpu.CompilerParams(vmem_limit_bytes=VMEM_LIMIT)
    whole, pair = (heads, TILE, TILE), (2 * heads, TILE, TILE)

    def call(kernel, name, out_shape, *operands, scratch=()):
        return pl.pallas_call(
            kernel,
            out_shape=[jax.ShapeDtypeStruct(shape, dtype) for shape, dtype in out_shape],
            in_specs=[vmem] * len(operands),
            out_specs=[vmem] * len(out_shape),
            scratch_shapes=list(scratch),
            compiler_params=params,
            name=name,
        )(*operands)

    rows = ((groups, 8, TILE), F32)
    (squares,) = call(functools.partial(squares_kernel, heads), "squares", [rows], q_raw, k_raw)
    sums = lax.all_to_all(squares, HEAD, 0, 0, tiled=True)
    q_norm, pairs, inverse = call(
        functools.partial(norm_kernel, heads, channels),
        "norm",
        [(whole, BF16), (pair, BF16), ((8, TILE), F32)],
        sums, q_raw, k_raw, values, gains,
    )
    tiles = spread(pairs) + [passed(pairs, line), passed(pairs, -line), half_round(pairs)]
    attended, dq, *parts = call(
        functools.partial(attention_kernel, heads),
        "attention",
        [(whole, BF16), (whole, F32)] + [(pair, F32 if t == 0 or 2 < t < near - 2 else BF16) for t in range(count)],
        q_norm, grad_out, *tiles,
        scratch=[pltpu.VMEM((heads, count, TILE, TILE), F32)],
    )
    arrived = collect(parts) + [
        passed(parts[near], -line), passed(parts[near + 1], line), half_round(parts[near + 2])
    ]
    dk, grad_v, terms = call(
        functools.partial(terms_kernel, heads),
        "terms",
        [(whole, F32), (whole, BF16), rows],
        q_raw, k_raw, dq, gains, parts[0], *arrived,
    )
    terms = lax.all_to_all(terms, HEAD, 0, 0, tiled=True)
    grad_q, grad_k = call(
        functools.partial(final_kernel, heads, channels),
        "final",
        [(whole, BF16)] * 2,
        inverse, terms, q_raw, k_raw, dq, dk, gains,
    )
    return tuple(
        jnp.transpose(array, (1, 0, 2)) for array in (attended, grad_q, grad_k, grad_v)
    )


def solution(mesh):
    split = Mesh(mesh.devices.reshape(4, -1, mesh.shape["head"] // 2, 2), SEQ + HEAD)

    def whole(q_raw, k_raw, values, grad_out, q_gain, k_gain, key_tiles):
        tokens = P(SEQ, HEAD, None)
        return jax.shard_map(
            functools.partial(per_device, q_raw.shape[1]),
            mesh=split,
            in_specs=(tokens,) * 4 + (P(HEAD, None), P(HEAD, None), P()),
            out_specs=(tokens,) * 4,
            check_vma=False,
        )(q_raw, k_raw, values, grad_out, q_gain, k_gain, key_tiles)

    return whole
```

```python
import functools

import jax
import jax.numpy as jnp
from jax import lax
from jax.experimental import pallas as pl
from jax.experimental.pallas import tpu as pltpu
from jax.sharding import Mesh, PartitionSpec as P

TILE = 128
EPS = 1e-06
NEAR = (0, -1, 1, -2, 2, -4, 4, -8, 8)
FAR = 3
NT = (((1,), (1,)), ((), ()))
NN = (((1,), (0,)), ((), ()))
TN = (((0,), (0,)), ((), ()))
F32 = jnp.float32
BF16 = jnp.bfloat16
VMEM_LIMIT = 24 * 1024 * 1024


def dot(left, right, dims):
    return lax.dot_general(left, right, dims, preferred_element_type=F32)


def row_sums(square):
    ones = jnp.ones((8, TILE), BF16)
    high = square.astype(BF16)
    low = (square - high.astype(F32)).astype(BF16)
    return dot(ones, high, NT) + dot(ones, low, NT)


def columns(rows):
    fill = jnp.zeros((TILE - rows.shape[0], TILE), F32)
    return jnp.transpose(jnp.concatenate([rows, fill], axis=0))


def own_frame():
    return lax.axis_index("x") * lax.axis_size("z") + lax.axis_index("z")


def mirrored(value):
    return value * (1 - 2 * lax.axis_index("c"))


def inside(place):
    line, lines = lax.axis_size("z"), lax.axis_size("x")
    near = len(NEAR)
    if place == 0 or place == near + FAR - 1:
        return None
    offset = NEAR[place] if place < near else (-line, line)[place - near]
    at = own_frame() + mirrored(offset)
    return (at >= 0) & (at < line * lines)


def squares_kernel(heads, q_ref, k_ref, out_ref):
    out_ref[...] = jnp.zeros(out_ref.shape, F32)
    for row, ref in enumerate((q_ref, k_ref)):
        total = jnp.zeros((TILE, TILE), F32)
        for head in range(heads):
            floats = ref[head].astype(F32)
            total = total + floats * floats
        total = row_sums(total)[0:1]
        for group in range(out_ref.shape[0]):
            out_ref[group, row : row + 1, :] = total


def group_sum(ref):
    total = ref[0]
    for group in range(1, ref.shape[0]):
        total = total + ref[group]
    return total


def norm_kernel(heads, channels, sums_ref, q_ref, k_ref, v_ref, gain_ref, qn_ref, kv_ref, inverse_ref):
    inverse = lax.rsqrt(group_sum(sums_ref) / channels + EPS)
    inverse_ref[...] = inverse
    turned = columns(inverse)
    for head in range(heads):
        qn_ref[head] = (
            q_ref[head].astype(F32) * turned[:, 0:1] * gain_ref[head : head + 1]
        ).astype(BF16)
        kv_ref[head] = (
            k_ref[head].astype(F32) * turned[:, 1:2] * gain_ref[heads + head : heads + head + 1]
        ).astype(BF16)
        kv_ref[heads + head] = v_ref[head]


def early_kernel(heads, places, q_ref, *refs):
    tiles, (weight_ref, out_ref, rows_ref) = refs[: len(places)], refs[len(places) :]
    scale = TILE ** (-0.5)
    usable = [inside(place) for place in places]
    lane = lax.broadcasted_iota(jnp.int32, (TILE, TILE), 1)
    rows = jnp.zeros((TILE, TILE), F32)
    tops = []
    for head in range(heads):
        top = jnp.full((TILE, TILE), -1e30, F32)
        for t, tile in enumerate(tiles):
            score = dot(q_ref[head], tile[head], NT) * scale
            if usable[t] is not None:
                score = jnp.where(usable[t], score, -1e30)
            weight_ref[head, t] = score
            top = jnp.maximum(top, score)
        tops.append(jnp.max(top, axis=1, keepdims=True))
        rows = jnp.where(lane == head, tops[head], rows)
    for head in range(heads):
        total = jnp.zeros((TILE, TILE), F32)
        out = jnp.zeros((TILE, TILE), F32)
        for t, tile in enumerate(tiles):
            weight = jnp.exp(weight_ref[head, t] - tops[head])
            weight_ref[head, t] = weight
            total = total + weight
            out = out + dot(weight.astype(BF16), tile[heads + head], NN)
        out_ref[head] = out
        rows = jnp.where(lane == heads + head, jnp.sum(total, axis=1, keepdims=True), rows)
    rows_ref[...] = rows


def late_kernel(heads, places, q_ref, do_ref, early_ref, rows_ref, *refs):
    count = len(places)
    tiles = refs[:count]
    out_ref, dq_ref, late_rows_ref = refs[count : count + 3]
    part_refs = refs[count + 3 :]
    scale = TILE ** (-0.5)
    usable = [inside(place) for place in places]
    lane = lax.broadcasted_iota(jnp.int32, (TILE, TILE), 1)
    rows = jnp.zeros((TILE, TILE), F32)
    for head in range(heads):
        query, upstream = q_ref[head], do_ref[head]
        early_top = rows_ref[:, head : head + 1]
        scores = []
        top = jnp.full((TILE, TILE), -1e30, F32)
        for t, tile in enumerate(tiles):
            score = dot(query, tile[head], NT) * scale
            score = jnp.where(usable[t], score, -1e30)
            scores.append(score)
            top = jnp.maximum(top, score)
        top = jnp.maximum(early_top, jnp.max(top, axis=1, keepdims=True))
        keep = jnp.exp(early_top - top)
        out = early_ref[head] * keep
        weights = [jnp.exp(score - top) for score in scores]
        total = weights[0]
        for weight in weights[1:]:
            total = total + weight
        total = jnp.sum(total, axis=1, keepdims=True)
        for t, tile in enumerate(tiles):
            out = out + dot(weights[t].astype(BF16), tile[heads + head], NN)
        share = 1.0 / (total + rows_ref[:, heads + head : heads + head + 1] * keep)
        out = (out * share).astype(BF16)
        out_ref[head] = out
        delta = jnp.sum(upstream.astype(F32) * out.astype(F32), axis=1, keepdims=True)
        query_grad = jnp.zeros((TILE, TILE), F32)
        for t, tile in enumerate(tiles):
            prob = weights[t] * share
            part = part_refs[t]
            part[heads + head] = dot(prob.astype(BF16), upstream, TN).astype(part.dtype)
            dscore = (prob * (dot(upstream, tile[heads + head], NT) - delta)).astype(BF16)
            part[head] = (dot(dscore, query, TN) * scale).astype(part.dtype)
            query_grad = query_grad + dot(dscore, tile[head], NN)
        dq_ref[head] = query_grad
        rows = jnp.where(lane == head, keep * share, rows)
        rows = jnp.where(lane == heads + head, delta, rows)
    late_rows_ref[...] = rows


def rest_kernel(heads, q_ref, do_ref, weight_ref, late_dq_ref, rows_ref, *refs):
    count = (len(refs) - 1) // 2
    tiles, dq_ref, part_refs = refs[:count], refs[count], refs[count + 1 :]
    scale = TILE ** (-0.5)
    for head in range(heads):
        query, upstream = q_ref[head], do_ref[head]
        share = rows_ref[:, head : head + 1]
        delta = rows_ref[:, heads + head : heads + head + 1]
        query_grad = late_dq_ref[head]
        for t, tile in enumerate(tiles):
            prob = weight_ref[head, t] * share
            part = part_refs[t]
            part[heads + head] = dot(prob.astype(BF16), upstream, TN).astype(part.dtype)
            dscore = (prob * (dot(upstream, tile[heads + head], NT) - delta)).astype(BF16)
            part[head] = (dot(dscore, query, TN) * scale).astype(part.dtype)
            query_grad = query_grad + dot(dscore, tile[head], NN)
        dq_ref[head] = query_grad * scale


def terms_kernel(heads, q_ref, k_ref, dq_ref, gain_ref, *refs):
    parts, (dk_ref, dv_ref, terms_ref) = refs[:-3], refs[-3:]
    query_total = jnp.zeros((TILE, TILE), F32)
    key_total = jnp.zeros((TILE, TILE), F32)
    for head in range(heads):
        key_grad, value_grad = parts[0][head], parts[0][heads + head]
        for part in parts[1:]:
            key_grad = key_grad + part[head].astype(F32)
            value_grad = value_grad + part[heads + head].astype(F32)
        dk_ref[head] = key_grad
        dv_ref[head] = value_grad.astype(BF16)
        query_total = query_total + q_ref[head].astype(F32) * (
            dq_ref[head] * gain_ref[head : head + 1]
        )
        key_total = key_total + k_ref[head].astype(F32) * (
            key_grad * gain_ref[heads + head : heads + head + 1]
        )
    terms_ref[...] = jnp.zeros(terms_ref.shape, F32)
    for row, total in enumerate((query_total, key_total)):
        total = row_sums(total)[0:1]
        for group in range(terms_ref.shape[0]):
            terms_ref[group, row : row + 1, :] = total


def final_kernel(
    heads, channels, inverse_ref, terms_ref, q_ref, k_ref, dq_ref, dk_ref, gain_ref, gq_ref, gk_ref
):
    inverse = inverse_ref[0:2]
    cubes = inverse * inverse * inverse * group_sum(terms_ref)[0:2] / channels
    turned = columns(jnp.concatenate([inverse, cubes], axis=0))
    for head in range(heads):
        gq_ref[head] = (
            turned[:, 0:1] * (gain_ref[head : head + 1] * dq_ref[head])
            - q_ref[head].astype(F32) * turned[:, 2:3]
        ).astype(BF16)
        gk_ref[head] = (
            turned[:, 1:2] * (gain_ref[heads + head : heads + head + 1] * dk_ref[head])
            - k_ref[head].astype(F32) * turned[:, 3:4]
        ).astype(BF16)


SEQ, HEAD = ("x", "z"), ("y", "c")


def passed(value, steps):
    count = lax.axis_size("x") * lax.axis_size("z")
    pairs = [
        (2 * i + core, 2 * (i + way * steps) + core)
        for i in range(count)
        for core, way in enumerate((1, -1))
        if 0 <= i + way * steps < count
    ]
    return lax.ppermute(value, SEQ + ("c",), pairs)


def half_round(value):
    count = lax.axis_size("x") * lax.axis_size("z")
    return lax.ppermute(value, SEQ, [(i, (i + count // 2) % count) for i in range(count)])


def relay(offset):
    return int(offset / 2) if abs(offset) > 2 else 0


def spread(value):
    got = {0: value}
    for offset in NEAR[1:]:
        got[offset] = passed(got[relay(offset)], relay(offset) - offset)
    return [got[offset] for offset in NEAR]


def collect(parts):
    places = [len(NEAR) - 2, len(NEAR) - 1]
    carried = [parts[place] for place in places]
    far = [parts[len(NEAR) + place] for place in range(FAR)]
    while True:
        steps = [NEAR[place] - relay(NEAR[place]) for place in places]
        through = relay(NEAR[places[0]])
        carried = [passed(part, step) for part, step in zip(carried, steps)]
        if not through:
            break
        places = [place - 2 for place in places]
        carried, far = lax.optimization_barrier((carried, far))
        carried = [
            (part.astype(F32) + parts[place]).astype(BF16) for part, place in zip(carried, places)
        ]
    line = lax.axis_size("z")
    return [
        *carried,
        *(passed(parts[place], NEAR[place]) for place in (1, 2)),
        passed(far[0], -line),
        passed(far[1], line),
        half_round(far[2]),
    ]


def per_device(total_heads, q_raw, k_raw, values, grad_out, q_gain, k_gain, key_tiles):
    line = lax.axis_size("z")
    groups = lax.axis_size("y") * lax.axis_size("c")
    near = len(NEAR)
    count = near + FAR
    heads = q_raw.shape[1]
    channels = float(total_heads * q_raw.shape[2])
    q_raw, k_raw, values, grad_out = [
        jnp.transpose(array, (1, 0, 2)) for array in (q_raw, k_raw, values, grad_out)
    ]
    gains = jnp.concatenate([q_gain, k_gain], axis=0)
    vmem = pl.BlockSpec(memory_space=pltpu.VMEM)
    params = pltpu.CompilerParams(vmem_limit_bytes=VMEM_LIMIT)
    whole, pair = (heads, TILE, TILE), (2 * heads, TILE, TILE)

    def call(kernel, name, out_shape, *operands, scratch=()):
        return pl.pallas_call(
            kernel,
            out_shape=[jax.ShapeDtypeStruct(shape, dtype) for shape, dtype in out_shape],
            in_specs=[vmem] * len(operands),
            out_specs=[vmem] * len(out_shape),
            scratch_shapes=list(scratch),
            compiler_params=params,
            name=name,
        )(*operands)

    rows = ((groups, 8, TILE), F32)
    (squares,) = call(functools.partial(squares_kernel, heads), "squares", [rows], q_raw, k_raw)
    sums = lax.all_to_all(squares, HEAD, 0, 0, tiled=True)
    q_norm, pairs, inverse = call(
        functools.partial(norm_kernel, heads, channels),
        "norm",
        [(whole, BF16), (pair, BF16), ((8, TILE), F32)],
        sums, q_raw, k_raw, values, gains,
    )
    tiles = spread(pairs) + [passed(pairs, line), passed(pairs, -line), half_round(pairs)]
    late = [near - 2, near - 1]
    early = [t for t in range(count) if t not in late]
    early_tiles, late_tiles = [tiles[t] for t in early], [tiles[t] for t in late]
    square = ((TILE, TILE), F32)
    weights, early_out, early_rows = call(
        functools.partial(early_kernel, heads, early),
        "early",
        [((heads, len(early), TILE, TILE), F32), (whole, F32), square],
        q_norm, *early_tiles,
    )
    attended, late_dq, late_rows, *late_parts = call(
        functools.partial(late_kernel, heads, late),
        "late",
        [(whole, BF16), (whole, F32), square] + [(pair, BF16)] * len(late),
        q_norm, grad_out, early_out, early_rows, *late_tiles,
    )
    dq, *early_parts = call(
        functools.partial(rest_kernel, heads),
        "rest",
        [(whole, F32)] + [(pair, F32 if t == 0 or 2 < t < near else BF16) for t in early],
        q_norm, grad_out, weights, late_dq, late_rows, *early_tiles,
    )
    parts = dict(zip(early + late, early_parts + late_parts))
    arrived = collect(parts)
    dk, grad_v, terms = call(
        functools.partial(terms_kernel, heads),
        "terms",
        [(whole, F32), (whole, BF16), rows],
        q_raw, k_raw, dq, gains, parts[0], *arrived,
    )
    terms = lax.all_to_all(terms, HEAD, 0, 0, tiled=True)
    grad_q, grad_k = call(
        functools.partial(final_kernel, heads, channels),
        "final",
        [(whole, BF16)] * 2,
        inverse, terms, q_raw, k_raw, dq, dk, gains,
    )
    return tuple(
        jnp.transpose(array, (1, 0, 2)) for array in (attended, grad_q, grad_k, grad_v)
    )


def solution(mesh):
    split = Mesh(mesh.devices.reshape(4, -1, mesh.shape["head"] // 2, 2), SEQ + HEAD)

    def whole(q_raw, k_raw, values, grad_out, q_gain, k_gain, key_tiles):
        tokens = P(SEQ, HEAD, None)
        return jax.shard_map(
            functools.partial(per_device, q_raw.shape[1]),
            mesh=split,
            in_specs=(tokens,) * 4 + (P(HEAD, None), P(HEAD, None), P()),
            out_specs=(tokens,) * 4,
            check_vma=False,
        )(q_raw, k_raw, values, grad_out, q_gain, k_gain, key_tiles)

    return whole
```

```python
import functools

import jax
import jax.numpy as jnp
from jax import lax
from jax.experimental import pallas as pl
from jax.experimental.pallas import tpu as pltpu
from jax.sharding import Mesh, PartitionSpec as P

TILE = 128
EPS = 1e-06
NEAR = (0, -1, 1, -2, 2, -4, 4, -8, 8)
FAR = 3
NT = (((1,), (1,)), ((), ()))
NN = (((1,), (0,)), ((), ()))
TN = (((0,), (0,)), ((), ()))
F32 = jnp.float32
BF16 = jnp.bfloat16
VMEM_LIMIT = 24 * 1024 * 1024


def dot(left, right, dims):
    return lax.dot_general(left, right, dims, preferred_element_type=F32)


def row_sums(square):
    ones = jnp.ones((8, TILE), BF16)
    high = square.astype(BF16)
    low = (square - high.astype(F32)).astype(BF16)
    return dot(ones, high, NT) + dot(ones, low, NT)


def columns(rows):
    fill = jnp.zeros((TILE - rows.shape[0], TILE), F32)
    return jnp.transpose(jnp.concatenate([rows, fill], axis=0))


def own_frame():
    return lax.axis_index("x") * lax.axis_size("z") + lax.axis_index("z")


def mirrored(value):
    return value * (1 - 2 * lax.axis_index("c"))


def inside(place):
    line, lines = lax.axis_size("z"), lax.axis_size("x")
    near = len(NEAR)
    if place == 0 or place == near + FAR - 1:
        return None
    offset = NEAR[place] if place < near else (-line, line)[place - near]
    at = own_frame() + mirrored(offset)
    return (at >= 0) & (at < line * lines)


def fetch(sources, targets, sems):
    copies = [
        pltpu.make_async_copy(source, target, sems.at[at])
        for at, (source, target) in enumerate(zip(sources, targets))
    ]
    for copy in copies:
        copy.start()
    for copy in copies:
        copy.wait()


def squares_kernel(heads, q_hbm, k_hbm, out_ref, q_ref, k_ref, sems):
    fetch((q_hbm, k_hbm), (q_ref, k_ref), sems)
    out_ref[...] = jnp.zeros(out_ref.shape, F32)
    for row, ref in enumerate((q_ref, k_ref)):
        total = jnp.zeros((TILE, TILE), F32)
        for head in range(heads):
            floats = ref[head].astype(F32)
            total = total + floats * floats
        total = row_sums(total)[0:1]
        for group in range(out_ref.shape[0]):
            out_ref[group, row : row + 1, :] = total


def group_sum(ref):
    total = ref[0]
    for group in range(1, ref.shape[0]):
        total = total + ref[group]
    return total


def norm_kernel(
    heads, channels, sums_ref, gain_ref, q_hbm, k_hbm, v_hbm, qn_ref, kv_ref, inverse_ref, q_ref, k_ref, sems
):
    fetch((q_hbm, k_hbm, v_hbm), (q_ref, k_ref, kv_ref.at[pl.ds(heads, heads)]), sems)
    inverse = lax.rsqrt(group_sum(sums_ref) / channels + EPS)
    inverse_ref[...] = inverse
    turned = columns(inverse)
    for head in range(heads):
        qn_ref[head] = (
            q_ref[head].astype(F32) * turned[:, 0:1] * gain_ref[head : head + 1]
        ).astype(BF16)
        kv_ref[head] = (
            k_ref[head].astype(F32) * turned[:, 1:2] * gain_ref[heads + head : heads + head + 1]
        ).astype(BF16)


def early_kernel(heads, places, q_ref, *refs):
    tiles, (weight_ref, out_ref, rows_ref) = refs[: len(places)], refs[len(places) :]
    scale = TILE ** (-0.5)
    usable = [inside(place) for place in places]
    lane = lax.broadcasted_iota(jnp.int32, (TILE, TILE), 1)
    rows = jnp.zeros((TILE, TILE), F32)
    tops = []
    for head in range(heads):
        top = jnp.full((TILE, TILE), -1e30, F32)
        for t, tile in enumerate(tiles):
            score = dot(q_ref[head], tile[head], NT) * scale
            if usable[t] is not None:
                score = jnp.where(usable[t], score, -1e30)
            weight_ref[head, t] = score
            top = jnp.maximum(top, score)
        tops.append(jnp.max(top, axis=1, keepdims=True))
        rows = jnp.where(lane == head, tops[head], rows)
    for head in range(heads):
        total = jnp.zeros((TILE, TILE), F32)
        out = jnp.zeros((TILE, TILE), F32)
        for t, tile in enumerate(tiles):
            weight = jnp.exp(weight_ref[head, t] - tops[head])
            weight_ref[head, t] = weight
            total = total + weight
            out = out + dot(weight.astype(BF16), tile[heads + head], NN)
        out_ref[head] = out
        rows = jnp.where(lane == heads + head, jnp.sum(total, axis=1, keepdims=True), rows)
    rows_ref[...] = rows


def late_kernel(heads, places, q_ref, do_ref, early_ref, rows_ref, *refs):
    count = len(places)
    tiles = refs[:count]
    out_ref, dq_ref, late_rows_ref = refs[count : count + 3]
    part_refs = refs[count + 3 :]
    scale = TILE ** (-0.5)
    usable = [inside(place) for place in places]
    lane = lax.broadcasted_iota(jnp.int32, (TILE, TILE), 1)
    rows = jnp.zeros((TILE, TILE), F32)
    every = range(heads)
    scores = [
        [jnp.where(use, dot(q_ref[head], tile[head], NT) * scale, -1e30) for use, tile in zip(usable, tiles)]
        for head in every
    ]
    dprobs = [[dot(do_ref[head], tile[heads + head], NT) for tile in tiles] for head in every]
    weights, keeps, shares, outs, deltas = [], [], [], [], []
    for head in every:
        early_top = rows_ref[:, head : head + 1]
        top = scores[head][0]
        for score in scores[head][1:]:
            top = jnp.maximum(top, score)
        top = jnp.maximum(early_top, jnp.max(top, axis=1, keepdims=True))
        keeps.append(jnp.exp(early_top - top))
        weights.append([jnp.exp(score - top) for score in scores[head]])
        total = weights[head][0]
        for weight in weights[head][1:]:
            total = total + weight
        total = jnp.sum(total, axis=1, keepdims=True)
        total = total + rows_ref[:, heads + head : heads + head + 1] * keeps[head]
        shares.append(1.0 / total)
    for head in every:
        out = early_ref[head] * keeps[head]
        for weight, tile in zip(weights[head], tiles):
            out = out + dot(weight.astype(BF16), tile[heads + head], NN)
        outs.append((out * shares[head]).astype(BF16))
        deltas.append(
            jnp.sum(do_ref[head].astype(F32) * outs[head].astype(F32), axis=1, keepdims=True)
        )
    probs = [[weight * shares[head] for weight in weights[head]] for head in every]
    dscores = [
        [(prob * (dprob - deltas[head])).astype(BF16) for prob, dprob in zip(probs[head], dprobs[head])]
        for head in every
    ]
    value_parts = [[dot(prob.astype(BF16), do_ref[head], TN) for prob in probs[head]] for head in every]
    key_parts = [[dot(dscore, q_ref[head], TN) * scale for dscore in dscores[head]] for head in every]
    for head in every:
        query_grad = jnp.zeros((TILE, TILE), F32)
        for dscore, tile in zip(dscores[head], tiles):
            query_grad = query_grad + dot(dscore, tile[head], NN)
        rows = jnp.where(lane == head, keeps[head] * shares[head], rows)
        rows = jnp.where(lane == heads + head, deltas[head], rows)
        for t, part in enumerate(part_refs):
            part[head] = key_parts[head][t].astype(part.dtype)
            part[heads + head] = value_parts[head][t].astype(part.dtype)
        out_ref[head] = outs[head]
        dq_ref[head] = query_grad
    late_rows_ref[...] = rows


def rest_kernel(heads, q_ref, do_ref, weight_ref, late_dq_ref, rows_ref, *refs):
    count = (len(refs) - 1) // 2
    tiles, dq_ref, part_refs = refs[:count], refs[count], refs[count + 1 :]
    scale = TILE ** (-0.5)
    for head in range(heads):
        query, upstream = q_ref[head], do_ref[head]
        share = rows_ref[:, head : head + 1]
        delta = rows_ref[:, heads + head : heads + head + 1]
        dprobs = [dot(upstream, tile[heads + head], NT) for tile in tiles]
        probs = [weight_ref[head, t] * share for t in range(count)]
        dscores = [(prob * (dprob - delta)).astype(BF16) for prob, dprob in zip(probs, dprobs)]
        query_grad = late_dq_ref[head]
        for dscore, tile in zip(dscores, tiles):
            query_grad = query_grad + dot(dscore, tile[head], NN)
        value_parts = [dot(prob.astype(BF16), upstream, TN) for prob in probs]
        key_parts = [dot(dscore, query, TN) * scale for dscore in dscores]
        for part, key_part, value_part in zip(part_refs, key_parts, value_parts):
            part[head] = key_part.astype(part.dtype)
            part[heads + head] = value_part.astype(part.dtype)
        dq_ref[head] = query_grad * scale


def terms_kernel(heads, q_ref, k_ref, dq_ref, gain_ref, *refs):
    parts, (dk_ref, dv_ref, terms_ref) = refs[:-3], refs[-3:]
    query_total = jnp.zeros((TILE, TILE), F32)
    key_total = jnp.zeros((TILE, TILE), F32)
    for head in range(heads):
        key_grad, value_grad = parts[0][head], parts[0][heads + head]
        for part in parts[1:]:
            key_grad = key_grad + part[head].astype(F32)
            value_grad = value_grad + part[heads + head].astype(F32)
        dk_ref[head] = key_grad
        dv_ref[head] = value_grad.astype(BF16)
        query_total = query_total + q_ref[head].astype(F32) * (
            dq_ref[head] * gain_ref[head : head + 1]
        )
        key_total = key_total + k_ref[head].astype(F32) * (
            key_grad * gain_ref[heads + head : heads + head + 1]
        )
    terms_ref[...] = jnp.zeros(terms_ref.shape, F32)
    for row, total in enumerate((query_total, key_total)):
        total = row_sums(total)[0:1]
        for group in range(terms_ref.shape[0]):
            terms_ref[group, row : row + 1, :] = total


def final_kernel(
    heads, channels, inverse_ref, terms_ref, q_ref, k_ref, dq_ref, dk_ref, gain_ref, gq_ref, gk_ref
):
    inverse = inverse_ref[0:2]
    cubes = inverse * inverse * inverse * group_sum(terms_ref)[0:2] / channels
    turned = columns(jnp.concatenate([inverse, cubes], axis=0))
    for head in range(heads):
        gq_ref[head] = (
            turned[:, 0:1] * (gain_ref[head : head + 1] * dq_ref[head])
            - q_ref[head].astype(F32) * turned[:, 2:3]
        ).astype(BF16)
        gk_ref[head] = (
            turned[:, 1:2] * (gain_ref[heads + head : heads + head + 1] * dk_ref[head])
            - k_ref[head].astype(F32) * turned[:, 3:4]
        ).astype(BF16)


SEQ, HEAD = ("x", "z"), ("y", "c")


def passed(value, steps):
    count = lax.axis_size("x") * lax.axis_size("z")
    pairs = [
        (2 * i + core, 2 * (i + way * steps) + core)
        for i in range(count)
        for core, way in enumerate((1, -1))
        if 0 <= i + way * steps < count
    ]
    return lax.ppermute(value, SEQ + ("c",), pairs)


def half_round(value):
    count = lax.axis_size("x") * lax.axis_size("z")
    return lax.ppermute(value, SEQ, [(i, (i + count // 2) % count) for i in range(count)])


def relay(offset):
    return int(offset / 2) if abs(offset) > 2 else 0


def spread(value):
    got = {0: value}
    for offset in NEAR[1:]:
        got[offset] = passed(got[relay(offset)], relay(offset) - offset)
    return [got[offset] for offset in NEAR]


def collect(parts):
    line = lax.axis_size("z")
    places = [len(NEAR) - 2, len(NEAR) - 1]
    carried = [parts[place] for place in places]
    others = [
        lambda: passed(parts[1], NEAR[1]),
        lambda: passed(parts[2], NEAR[2]),
        lambda: half_round(parts[len(NEAR) + 2]),
        lambda: passed(parts[len(NEAR)], -line),
        lambda: passed(parts[len(NEAR) + 1], line),
    ]
    arrived = []
    while True:
        steps = [NEAR[place] - relay(NEAR[place]) for place in places]
        through = relay(NEAR[places[0]])
        carried = [passed(part, step) for part, step in zip(carried, steps)]
        if not through:
            break
        places = [place - 2 for place in places]
        carried = lax.optimization_barrier(carried)
        carried = [
            (part.astype(F32) + parts[place]).astype(BF16) for part, place in zip(carried, places)
        ]
        arrived += [send() for send in others[:3]]
        others = others[3:]
        carried, arrived = lax.optimization_barrier((carried, arrived))
    return carried + arrived + [send() for send in others]


def per_device(total_heads, q_raw, k_raw, values, grad_out, q_gain, k_gain, key_tiles):
    line = lax.axis_size("z")
    groups = lax.axis_size("y") * lax.axis_size("c")
    near = len(NEAR)
    count = near + FAR
    heads = q_raw.shape[1]
    channels = float(total_heads * q_raw.shape[2])
    q_raw, k_raw, values, grad_out = [
        jnp.transpose(array, (1, 0, 2)) for array in (q_raw, k_raw, values, grad_out)
    ]
    gains = jnp.concatenate([q_gain, k_gain], axis=0)
    vmem = pl.BlockSpec(memory_space=pltpu.VMEM)
    params = pltpu.CompilerParams(vmem_limit_bytes=VMEM_LIMIT)
    whole, pair = (heads, TILE, TILE), (2 * heads, TILE, TILE)

    def call(kernel, name, out_shape, *operands, scratch=(), raw=0):
        return pl.pallas_call(
            kernel,
            out_shape=[jax.ShapeDtypeStruct(shape, dtype) for shape, dtype in out_shape],
            in_specs=[vmem] * (len(operands) - raw) + [pl.BlockSpec(memory_space=pltpu.HBM)] * raw,
            out_specs=[vmem] * len(out_shape),
            scratch_shapes=list(scratch),
            compiler_params=params,
            name=name,
        )(*operands)

    rows = ((groups, 8, TILE), F32)
    held = [pltpu.VMEM(whole, BF16)] * 2
    (squares,) = call(
        functools.partial(squares_kernel, heads),
        "squares",
        [rows],
        q_raw, k_raw,
        scratch=held + [pltpu.SemaphoreType.DMA((2,))],
        raw=2,
    )
    sums = lax.all_to_all(squares, HEAD, 0, 0, tiled=True)
    q_norm, pairs, inverse = call(
        functools.partial(norm_kernel, heads, channels),
        "norm",
        [(whole, BF16), (pair, BF16), ((8, TILE), F32)],
        sums, gains, q_raw, k_raw, values,
        scratch=held + [pltpu.SemaphoreType.DMA((3,))],
        raw=3,
    )
    tiles = spread(pairs) + [passed(pairs, line), passed(pairs, -line), half_round(pairs)]
    late = [near - 2, near - 1]
    early = [t for t in range(count) if t not in late]
    early_tiles, late_tiles = [tiles[t] for t in early], [tiles[t] for t in late]
    square = ((TILE, TILE), F32)
    weights, early_out, early_rows = call(
        functools.partial(early_kernel, heads, early),
        "early",
        [((heads, len(early), TILE, TILE), F32), (whole, F32), square],
        q_norm, *early_tiles,
    )
    attended, late_dq, late_rows, *late_parts = call(
        functools.partial(late_kernel, heads, late),
        "late",
        [(whole, BF16), (whole, F32), square] + [(pair, BF16)] * len(late),
        q_norm, grad_out, early_out, early_rows, *late_tiles,
    )
    dq, *early_parts = call(
        functools.partial(rest_kernel, heads),
        "rest",
        [(whole, F32)] + [(pair, F32 if t == 0 or 2 < t < near else BF16) for t in early],
        q_norm, grad_out, weights, late_dq, late_rows, *early_tiles,
    )
    parts = dict(zip(early + late, early_parts + late_parts))
    arrived = collect(parts)
    dk, grad_v, terms = call(
        functools.partial(terms_kernel, heads),
        "terms",
        [(whole, F32), (whole, BF16), rows],
        q_raw, k_raw, dq, gains, parts[0], *arrived,
    )
    terms = lax.all_to_all(terms, HEAD, 0, 0, tiled=True)
    grad_q, grad_k = call(
        functools.partial(final_kernel, heads, channels),
        "final",
        [(whole, BF16)] * 2,
        inverse, terms, q_raw, k_raw, dq, dk, gains,
    )
    return tuple(
        jnp.transpose(array, (1, 0, 2)) for array in (attended, grad_q, grad_k, grad_v)
    )


def solution(mesh):
    split = Mesh(mesh.devices.reshape(4, -1, mesh.shape["head"] // 2, 2), SEQ + HEAD)

    def whole(q_raw, k_raw, values, grad_out, q_gain, k_gain, key_tiles):
        tokens = P(SEQ, HEAD, None)
        return jax.shard_map(
            functools.partial(per_device, q_raw.shape[1]),
            mesh=split,
            in_specs=(tokens,) * 4 + (P(HEAD, None), P(HEAD, None), P()),
            out_specs=(tokens,) * 4,
            check_vma=False,
        )(q_raw, k_raw, values, grad_out, q_gain, k_gain, key_tiles)

    return whole
```

```python
import functools

import jax
import jax.numpy as jnp
from jax import lax
from jax.experimental import pallas as pl
from jax.experimental.pallas import tpu as pltpu
from jax.sharding import Mesh, PartitionSpec as P

TILE = 128
EPS = 1e-06
NEAR = (0, -1, 1, -2, 2, -4, 4, -8, 8)
FAR = 3
NT = (((1,), (1,)), ((), ()))
NN = (((1,), (0,)), ((), ()))
TN = (((0,), (0,)), ((), ()))
F32 = jnp.float32
BF16 = jnp.bfloat16
VMEM_LIMIT = 24 * 1024 * 1024


def dot(left, right, dims):
    return lax.dot_general(left, right, dims, preferred_element_type=F32)


def row_sums(square):
    ones = jnp.ones((8, TILE), BF16)
    high = square.astype(BF16)
    low = (square - high.astype(F32)).astype(BF16)
    return dot(ones, high, NT) + dot(ones, low, NT)


def columns(rows):
    fill = jnp.zeros((TILE - rows.shape[0], TILE), F32)
    return jnp.transpose(jnp.concatenate([rows, fill], axis=0))


def own_frame():
    return lax.axis_index("x") * lax.axis_size("z") + lax.axis_index("z")


def mirrored(value):
    return value * (1 - 2 * lax.axis_index("c"))


def inside(place):
    line, lines = lax.axis_size("z"), lax.axis_size("x")
    near = len(NEAR)
    if place == 0 or place == near + FAR - 1:
        return None
    offset = NEAR[place] if place < near else (-line, line)[place - near]
    at = own_frame() + mirrored(offset)
    return (at >= 0) & (at < line * lines)


def squares_kernel(heads, raw_ref, out_ref):
    out_ref[...] = jnp.zeros(out_ref.shape, F32)
    for row in range(2):
        total = jnp.zeros((TILE, TILE), F32)
        for head in range(heads):
            floats = raw_ref[row * heads + head].astype(F32)
            total = total + floats * floats
        total = row_sums(total)[0:1]
        for group in range(out_ref.shape[0]):
            out_ref[group, row : row + 1, :] = total


def group_sum(ref):
    total = ref[0]
    for group in range(1, ref.shape[0]):
        total = total + ref[group]
    return total


def norm_kernel(heads, channels, sums_ref, gain_ref, raw_ref, qn_ref, kv_ref, inverse_ref):
    inverse = lax.rsqrt(group_sum(sums_ref) / channels + EPS)
    inverse_ref[...] = inverse
    turned = columns(inverse)
    for head in range(heads):
        qn_ref[head] = (
            raw_ref[head].astype(F32) * turned[:, 0:1] * gain_ref[head : head + 1]
        ).astype(BF16)
        kv_ref[heads + head] = raw_ref[2 * heads + head]
        kv_ref[head] = (
            raw_ref[heads + head].astype(F32) * turned[:, 1:2] * gain_ref[heads + head : heads + head + 1]
        ).astype(BF16)


def early_kernel(heads, places, q_ref, *refs):
    tiles, (weight_ref, out_ref, rows_ref) = refs[: len(places)], refs[len(places) :]
    scale = TILE ** (-0.5)
    usable = [inside(place) for place in places]
    lane = lax.broadcasted_iota(jnp.int32, (TILE, TILE), 1)
    rows = jnp.zeros((TILE, TILE), F32)
    tops = []
    for head in range(heads):
        top = jnp.full((TILE, TILE), -1e30, F32)
        for t, tile in enumerate(tiles):
            score = dot(q_ref[head], tile[head], NT) * scale
            if usable[t] is not None:
                score = jnp.where(usable[t], score, -1e30)
            weight_ref[head, t] = score
            top = jnp.maximum(top, score)
        tops.append(jnp.max(top, axis=1, keepdims=True))
        rows = jnp.where(lane == head, tops[head], rows)
    for head in range(heads):
        total = jnp.zeros((TILE, TILE), F32)
        out = jnp.zeros((TILE, TILE), F32)
        for t, tile in enumerate(tiles):
            weight = jnp.exp(weight_ref[head, t] - tops[head])
            weight_ref[head, t] = weight
            total = total + weight
            out = out + dot(weight.astype(BF16), tile[heads + head], NN)
        out_ref[head] = out
        rows = jnp.where(lane == heads + head, jnp.sum(total, axis=1, keepdims=True), rows)
    rows_ref[...] = rows


def late_kernel(heads, places, q_ref, do_ref, early_ref, rows_ref, *refs):
    count = len(places)
    tiles = refs[:count]
    out_ref, dq_ref, late_rows_ref = refs[count : count + 3]
    part_refs = refs[count + 3 :]
    scale = TILE ** (-0.5)
    usable = [inside(place) for place in places]
    lane = lax.broadcasted_iota(jnp.int32, (TILE, TILE), 1)
    rows = jnp.zeros((TILE, TILE), F32)
    every = range(heads)
    scores = [
        [dot(q_ref[head], tile[head], NT) * scale for tile in tiles] for head in every
    ]
    scores = [
        [score if use is None else jnp.where(use, score, -1e30) for use, score in zip(usable, row)]
        for row in scores
    ]
    dprobs = [[dot(do_ref[head], tile[heads + head], NT) for tile in tiles] for head in every]
    weights, keeps, shares, outs, deltas = [], [], [], [], []
    for head in every:
        early_top = rows_ref[:, head : head + 1]
        top = scores[head][0]
        for score in scores[head][1:]:
            top = jnp.maximum(top, score)
        top = jnp.maximum(early_top, jnp.max(top, axis=1, keepdims=True))
        keeps.append(jnp.exp(early_top - top))
        weights.append([jnp.exp(score - top) for score in scores[head]])
        total = weights[head][0]
        for weight in weights[head][1:]:
            total = total + weight
        total = jnp.sum(total, axis=1, keepdims=True)
        total = total + rows_ref[:, heads + head : heads + head + 1] * keeps[head]
        shares.append(1.0 / total)
    for head in every:
        out = early_ref[head] * keeps[head]
        for weight, tile in zip(weights[head], tiles):
            out = out + dot(weight.astype(BF16), tile[heads + head], NN)
        outs.append((out * shares[head]).astype(BF16))
        deltas.append(
            jnp.sum(do_ref[head].astype(F32) * outs[head].astype(F32), axis=1, keepdims=True)
        )
    probs = [[weight * shares[head] for weight in weights[head]] for head in every]
    dscores = [
        [(prob * (dprob - deltas[head])).astype(BF16) for prob, dprob in zip(probs[head], dprobs[head])]
        for head in every
    ]
    value_parts = [[dot(prob.astype(BF16), do_ref[head], TN) for prob in probs[head]] for head in every]
    key_parts = [[dot(dscore, q_ref[head], TN) * scale for dscore in dscores[head]] for head in every]
    for head in every:
        query_grad = jnp.zeros((TILE, TILE), F32)
        for dscore, tile in zip(dscores[head], tiles):
            query_grad = query_grad + dot(dscore, tile[head], NN)
        rows = jnp.where(lane == head, keeps[head] * shares[head], rows)
        rows = jnp.where(lane == heads + head, deltas[head], rows)
        for t, part in enumerate(part_refs):
            part[head] = key_parts[head][t].astype(part.dtype)
            part[heads + head] = value_parts[head][t].astype(part.dtype)
        out_ref[head] = outs[head]
        dq_ref[head] = query_grad
    late_rows_ref[...] = rows


def rest_kernel(heads, q_ref, do_ref, weight_ref, late_dq_ref, rows_ref, *refs):
    count = (len(refs) - 1) // 2
    tiles, dq_ref, part_refs = refs[:count], refs[count], refs[count + 1 :]
    scale = TILE ** (-0.5)
    for head in range(heads):
        query, upstream = q_ref[head], do_ref[head]
        share = rows_ref[:, head : head + 1]
        delta = rows_ref[:, heads + head : heads + head + 1]
        dprobs = [dot(upstream, tile[heads + head], NT) for tile in tiles]
        probs = [weight_ref[head, t] * share for t in range(count)]
        dscores = [(prob * (dprob - delta)).astype(BF16) for prob, dprob in zip(probs, dprobs)]
        query_grad = late_dq_ref[head]
        for dscore, tile in zip(dscores, tiles):
            query_grad = query_grad + dot(dscore, tile[head], NN)
        value_parts = [dot(prob.astype(BF16), upstream, TN) for prob in probs]
        key_parts = [dot(dscore, query, TN) * scale for dscore in dscores]
        for part, key_part, value_part in zip(part_refs, key_parts, value_parts):
            part[head] = key_part.astype(part.dtype)
            part[heads + head] = value_part.astype(part.dtype)
        dq_ref[head] = query_grad * scale


def terms_kernel(heads, raw_ref, dq_ref, gain_ref, *refs):
    parts, (dk_ref, dv_ref, terms_ref) = refs[:-3], refs[-3:]
    query_total = jnp.zeros((TILE, TILE), F32)
    key_total = jnp.zeros((TILE, TILE), F32)
    for head in range(heads):
        key_grad, value_grad = parts[0][head], parts[0][heads + head]
        for part in parts[1:]:
            key_grad = key_grad + part[head].astype(F32)
            value_grad = value_grad + part[heads + head].astype(F32)
        dk_ref[head] = key_grad
        dv_ref[head] = value_grad.astype(BF16)
        query_total = query_total + raw_ref[head].astype(F32) * (
            dq_ref[head] * gain_ref[head : head + 1]
        )
        key_total = key_total + raw_ref[heads + head].astype(F32) * (
            key_grad * gain_ref[heads + head : heads + head + 1]
        )
    terms_ref[...] = jnp.zeros(terms_ref.shape, F32)
    for row, total in enumerate((query_total, key_total)):
        total = row_sums(total)[0:1]
        for group in range(terms_ref.shape[0]):
            terms_ref[group, row : row + 1, :] = total


def final_kernel(
    heads, channels, inverse_ref, terms_ref, raw_ref, dq_ref, dk_ref, gain_ref, gq_ref, gk_ref
):
    inverse = inverse_ref[0:2]
    cubes = inverse * inverse * inverse * group_sum(terms_ref)[0:2] / channels
    turned = columns(jnp.concatenate([inverse, cubes], axis=0))
    for head in range(heads):
        gq_ref[head] = (
            turned[:, 0:1] * (gain_ref[head : head + 1] * dq_ref[head])
            - raw_ref[head].astype(F32) * turned[:, 2:3]
        ).astype(BF16)
        gk_ref[head] = (
            turned[:, 1:2] * (gain_ref[heads + head : heads + head + 1] * dk_ref[head])
            - raw_ref[heads + head].astype(F32) * turned[:, 3:4]
        ).astype(BF16)


SEQ, HEAD = ("x", "z"), ("y", "c")


def passed(value, steps):
    count = lax.axis_size("x") * lax.axis_size("z")
    pairs = [
        (2 * i + core, 2 * (i + way * steps) + core)
        for i in range(count)
        for core, way in enumerate((1, -1))
        if 0 <= i + way * steps < count
    ]
    return lax.ppermute(value, SEQ + ("c",), pairs)


def half_round(value):
    count = lax.axis_size("x") * lax.axis_size("z")
    return lax.ppermute(value, SEQ, [(i, (i + count // 2) % count) for i in range(count)])


def relay(offset):
    return int(offset / 2) if abs(offset) > 2 else 0


def spread(value):
    got = {0: value}
    for offset in NEAR[1:]:
        got[offset] = passed(got[relay(offset)], relay(offset) - offset)
    return [got[offset] for offset in NEAR]


def collect(parts):
    line = lax.axis_size("z")
    places = [len(NEAR) - 2, len(NEAR) - 1]
    carried = [parts[place] for place in places]
    others = [
        lambda: parts[0] + half_round(parts[len(NEAR) + 2]).astype(F32),
        lambda: passed(parts[1], NEAR[1]),
        lambda: passed(parts[2], NEAR[2]),
        lambda: passed(parts[len(NEAR)], -line),
        lambda: passed(parts[len(NEAR) + 1], line),
    ]
    arrived = []
    while True:
        steps = [NEAR[place] - relay(NEAR[place]) for place in places]
        through = relay(NEAR[places[0]])
        carried = [passed(part, step) for part, step in zip(carried, steps)]
        if not through:
            break
        places = [place - 2 for place in places]
        carried = lax.optimization_barrier(carried)
        carried = [
            (part.astype(F32) + parts[place]).astype(BF16) for part, place in zip(carried, places)
        ]
        arrived += [send() for send in others[:3]]
        others = others[3:]
        carried, arrived = lax.optimization_barrier((carried, arrived))
    return arrived + carried + [send() for send in others]


def per_device(total_heads, q_raw, k_raw, values, grad_out, q_gain, k_gain, key_tiles):
    line = lax.axis_size("z")
    groups = lax.axis_size("y") * lax.axis_size("c")
    near = len(NEAR)
    count = near + FAR
    heads = q_raw.shape[1]
    channels = float(total_heads * q_raw.shape[2])
    q_raw, k_raw, values, grad_out = [
        jnp.transpose(array, (1, 0, 2)) for array in (q_raw, k_raw, values, grad_out)
    ]
    gains = jnp.concatenate([q_gain, k_gain], axis=0)
    vmem = pl.BlockSpec(memory_space=pltpu.VMEM)
    params = pltpu.CompilerParams(vmem_limit_bytes=VMEM_LIMIT)
    whole, pair = (heads, TILE, TILE), (2 * heads, TILE, TILE)

    def call(kernel, name, out_shape, *operands):
        return pl.pallas_call(
            kernel,
            out_shape=[jax.ShapeDtypeStruct(shape, dtype) for shape, dtype in out_shape],
            in_specs=[vmem] * len(operands),
            out_specs=[vmem] * len(out_shape),
            compiler_params=params,
            name=name,
        )(*operands)

    rows = ((groups, 8, TILE), F32)
    raw = jnp.concatenate([q_raw, k_raw, values], axis=0)
    (squares,) = call(functools.partial(squares_kernel, heads), "squares", [rows], raw)
    sums = lax.all_to_all(squares, HEAD, 0, 0, tiled=True)
    q_norm, pairs, inverse = call(
        functools.partial(norm_kernel, heads, channels),
        "norm",
        [(whole, BF16), (pair, BF16), ((8, TILE), F32)],
        sums, gains, raw,
    )
    half = half_round(pairs)
    tiles = spread(pairs)
    tiles += [passed(pairs, line), passed(pairs, -line), half]
    late = [near - 2, near - 1]
    early = [t for t in range(count) if t not in late]
    early_tiles, late_tiles = [tiles[t] for t in early], [tiles[t] for t in late]
    square = ((TILE, TILE), F32)
    weights, early_out, early_rows = call(
        functools.partial(early_kernel, heads, early),
        "early",
        [((heads, len(early), TILE, TILE), F32), (whole, F32), square],
        q_norm, *early_tiles,
    )
    attended, late_dq, late_rows, *late_parts = call(
        functools.partial(late_kernel, heads, late),
        "late",
        [(whole, BF16), (whole, F32), square] + [(pair, BF16)] * len(late),
        q_norm, grad_out, early_out, early_rows, *late_tiles,
    )
    dq, *early_parts = call(
        functools.partial(rest_kernel, heads),
        "rest",
        [(whole, F32)] + [(pair, F32 if t == 0 or 2 < t < near else BF16) for t in early],
        q_norm, grad_out, weights, late_dq, late_rows, *early_tiles,
    )
    parts = dict(zip(early + late, early_parts + late_parts))
    arrived = collect(parts)
    dk, grad_v, terms = call(
        functools.partial(terms_kernel, heads),
        "terms",
        [(whole, F32), (whole, BF16), rows],
        raw, dq, gains, *arrived,
    )
    terms = lax.all_to_all(terms, HEAD, 0, 0, tiled=True)
    grad_q, grad_k = call(
        functools.partial(final_kernel, heads, channels),
        "final",
        [(whole, BF16)] * 2,
        inverse, terms, raw, dq, dk, gains,
    )
    return tuple(
        jnp.transpose(array, (1, 0, 2)) for array in (attended, grad_q, grad_k, grad_v)
    )


def solution(mesh):
    split = Mesh(mesh.devices.reshape(4, -1, mesh.shape["head"] // 2, 2), SEQ + HEAD)

    def whole(q_raw, k_raw, values, grad_out, q_gain, k_gain, key_tiles):
        tokens = P(SEQ, HEAD, None)
        return jax.shard_map(
            functools.partial(per_device, q_raw.shape[1]),
            mesh=split,
            in_specs=(tokens,) * 4 + (P(HEAD, None), P(HEAD, None), P()),
            out_specs=(tokens,) * 4,
            check_vma=False,
        )(q_raw, k_raw, values, grad_out, q_gain, k_gain, key_tiles)

    return whole
```

```python
import functools

import jax
import jax.numpy as jnp
from jax import lax
from jax.experimental import pallas as pl
from jax.experimental.pallas import tpu as pltpu
from jax.sharding import Mesh, PartitionSpec as P

TILE = 128
EPS = 1e-06
NEAR = (0, -1, 1, -2, 2, -4, 4, -8, 8)
FAR = 3
NT = (((1,), (1,)), ((), ()))
NN = (((1,), (0,)), ((), ()))
TN = (((0,), (0,)), ((), ()))
F32 = jnp.float32
BF16 = jnp.bfloat16
VMEM_LIMIT = 24 * 1024 * 1024


def dot(left, right, dims):
    return lax.dot_general(left, right, dims, preferred_element_type=F32)


def row_sums(square):
    ones = jnp.ones((8, TILE), BF16)
    high = square.astype(BF16)
    low = (square - high.astype(F32)).astype(BF16)
    return dot(ones, high, NT) + dot(ones, low, NT)


def columns(rows):
    fill = jnp.zeros((TILE - rows.shape[0], TILE), F32)
    return jnp.transpose(jnp.concatenate([rows, fill], axis=0))


def own_frame():
    return lax.axis_index("x") * lax.axis_size("z") + lax.axis_index("z")


def mirrored(value):
    return value * (1 - 2 * lax.axis_index("c"))


def inside(place):
    line, lines = lax.axis_size("z"), lax.axis_size("x")
    near = len(NEAR)
    if place == 0 or place == near + FAR - 1:
        return None
    offset = NEAR[place] if place < near else (-line, line)[place - near]
    at = own_frame() + mirrored(offset)
    return (at >= 0) & (at < line * lines)


def squares_kernel(heads, raw_ref, out_ref):
    out_ref[...] = jnp.zeros(out_ref.shape, F32)
    for row in range(2):
        total = jnp.zeros((TILE, TILE), F32)
        for head in range(heads):
            floats = raw_ref[row * heads + head].astype(F32)
            total = total + floats * floats
        total = row_sums(total)[0:1]
        for group in range(out_ref.shape[0]):
            out_ref[group, row : row + 1, :] = total


def group_sum(ref):
    total = ref[0]
    for group in range(1, ref.shape[0]):
        total = total + ref[group]
    return total


def norm_kernel(heads, channels, sums_ref, gain_ref, raw_ref, qn_ref, kv_ref, inverse_ref):
    inverse = lax.rsqrt(group_sum(sums_ref) / channels + EPS)
    inverse_ref[...] = inverse
    turned = columns(inverse)
    for head in range(heads):
        qn_ref[head] = (
            raw_ref[head].astype(F32) * turned[:, 0:1] * gain_ref[head : head + 1]
        ).astype(BF16)
        kv_ref[heads + head] = raw_ref[2 * heads + head]
        kv_ref[head] = (
            raw_ref[heads + head].astype(F32) * turned[:, 1:2] * gain_ref[heads + head : heads + head + 1]
        ).astype(BF16)


def early_kernel(heads, places, q_ref, *refs):
    tiles, (weight_ref, out_ref, rows_ref) = refs[: len(places)], refs[len(places) :]
    scale = TILE ** (-0.5)
    usable = [inside(place) for place in places]
    lane = lax.broadcasted_iota(jnp.int32, (TILE, TILE), 1)
    rows = jnp.zeros((TILE, TILE), F32)
    tops = []
    for head in range(heads):
        top = jnp.full((TILE, TILE), -1e30, F32)
        for t, tile in enumerate(tiles):
            score = dot(q_ref[head], tile[head], NT) * scale
            if usable[t] is not None:
                score = jnp.where(usable[t], score, -1e30)
            weight_ref[head, t] = score
            top = jnp.maximum(top, score)
        tops.append(jnp.max(top, axis=1, keepdims=True))
        rows = jnp.where(lane == head, tops[head], rows)
    for head in range(heads):
        total = jnp.zeros((TILE, TILE), F32)
        out = jnp.zeros((TILE, TILE), F32)
        for t, tile in enumerate(tiles):
            weight = jnp.exp(weight_ref[head, t] - tops[head])
            weight_ref[head, t] = weight
            total = total + weight
            out = out + dot(weight.astype(BF16), tile[heads + head], NN)
        out_ref[head] = out
        rows = jnp.where(lane == heads + head, jnp.sum(total, axis=1, keepdims=True), rows)
    rows_ref[...] = rows


def late_kernel(heads, places, q_ref, do_ref, early_ref, rows_ref, *refs):
    count = len(places)
    tiles = refs[:count]
    out_ref, dq_ref, late_rows_ref = refs[count : count + 3]
    part_refs = refs[count + 3 :]
    scale = TILE ** (-0.5)
    usable = [inside(place) for place in places]
    lane = lax.broadcasted_iota(jnp.int32, (TILE, TILE), 1)
    rows = jnp.zeros((TILE, TILE), F32)
    every = range(heads)
    scores = [
        [dot(q_ref[head], tile[head], NT) * scale for tile in tiles] for head in every
    ]
    scores = [
        [score if use is None else jnp.where(use, score, -1e30) for use, score in zip(usable, row)]
        for row in scores
    ]
    dprobs = [[dot(do_ref[head], tile[heads + head], NT) for tile in tiles] for head in every]
    weights, keeps, shares, outs, deltas = [], [], [], [], []
    for head in every:
        early_top = rows_ref[:, head : head + 1]
        top = scores[head][0]
        for score in scores[head][1:]:
            top = jnp.maximum(top, score)
        top = jnp.maximum(early_top, jnp.max(top, axis=1, keepdims=True))
        keeps.append(jnp.exp(early_top - top))
        weights.append([jnp.exp(score - top) for score in scores[head]])
        total = weights[head][0]
        for weight in weights[head][1:]:
            total = total + weight
        total = jnp.sum(total, axis=1, keepdims=True)
        total = total + rows_ref[:, heads + head : heads + head + 1] * keeps[head]
        shares.append(1.0 / total)
    for head in every:
        out = early_ref[head] * keeps[head]
        for weight, tile in zip(weights[head], tiles):
            out = out + dot(weight.astype(BF16), tile[heads + head], NN)
        outs.append((out * shares[head]).astype(BF16))
        deltas.append(
            jnp.sum(do_ref[head].astype(F32) * outs[head].astype(F32), axis=1, keepdims=True)
        )
    probs = [[weight * shares[head] for weight in weights[head]] for head in every]
    dscores = [
        [(prob * (dprob - deltas[head])).astype(BF16) for prob, dprob in zip(probs[head], dprobs[head])]
        for head in every
    ]
    value_parts = [[dot(prob.astype(BF16), do_ref[head], TN) for prob in probs[head]] for head in every]
    key_parts = [[dot(dscore, q_ref[head], TN) * scale for dscore in dscores[head]] for head in every]
    for head in every:
        query_grad = jnp.zeros((TILE, TILE), F32)
        for dscore, tile in zip(dscores[head], tiles):
            query_grad = query_grad + dot(dscore, tile[head], NN)
        rows = jnp.where(lane == head, keeps[head] * shares[head], rows)
        rows = jnp.where(lane == heads + head, deltas[head], rows)
        for t, part in enumerate(part_refs):
            part[head] = key_parts[head][t].astype(part.dtype)
            part[heads + head] = value_parts[head][t].astype(part.dtype)
        out_ref[head] = outs[head]
        dq_ref[head] = query_grad
    late_rows_ref[...] = rows


def rest_kernel(heads, q_ref, do_ref, weight_ref, late_dq_ref, rows_ref, *refs):
    count = (len(refs) - 1) // 2
    tiles, dq_ref, part_refs = refs[:count], refs[count], refs[count + 1 :]
    scale = TILE ** (-0.5)
    for head in range(heads):
        query, upstream = q_ref[head], do_ref[head]
        share = rows_ref[:, head : head + 1]
        delta = rows_ref[:, heads + head : heads + head + 1]
        dprobs = [dot(upstream, tile[heads + head], NT) for tile in tiles]
        probs = [weight_ref[head, t] * share for t in range(count)]
        dscores = [(prob * (dprob - delta)).astype(BF16) for prob, dprob in zip(probs, dprobs)]
        query_grad = late_dq_ref[head]
        for dscore, tile in zip(dscores, tiles):
            query_grad = query_grad + dot(dscore, tile[head], NN)
        value_parts = [dot(prob.astype(BF16), upstream, TN) for prob in probs]
        key_parts = [dot(dscore, query, TN) * scale for dscore in dscores]
        for part, key_part, value_part in zip(part_refs, key_parts, value_parts):
            part[head] = key_part.astype(part.dtype)
            part[heads + head] = value_part.astype(part.dtype)
        dq_ref[head] = query_grad * scale


def terms_kernel(heads, raw_ref, dq_ref, gain_ref, *refs):
    parts, (dk_ref, dv_ref, terms_ref) = refs[:-3], refs[-3:]
    query_total = jnp.zeros((TILE, TILE), F32)
    key_total = jnp.zeros((TILE, TILE), F32)
    for head in range(heads):
        key_grad, value_grad = parts[0][head], parts[0][heads + head]
        for part in parts[1:]:
            key_grad = key_grad + part[head].astype(F32)
            value_grad = value_grad + part[heads + head].astype(F32)
        dk_ref[head] = key_grad
        dv_ref[head] = value_grad.astype(BF16)
        query_total = query_total + raw_ref[head].astype(F32) * (
            dq_ref[head] * gain_ref[head : head + 1]
        )
        key_total = key_total + raw_ref[heads + head].astype(F32) * (
            key_grad * gain_ref[heads + head : heads + head + 1]
        )
    terms_ref[...] = jnp.zeros(terms_ref.shape, F32)
    for row, total in enumerate((query_total, key_total)):
        total = row_sums(total)[0:1]
        for group in range(terms_ref.shape[0]):
            terms_ref[group, row : row + 1, :] = total


def final_kernel(
    heads, channels, inverse_ref, terms_ref, raw_ref, dq_ref, dk_ref, gain_ref, gq_ref, gk_ref
):
    inverse = inverse_ref[0:2]
    cubes = inverse * inverse * inverse * group_sum(terms_ref)[0:2] / channels
    turned = columns(jnp.concatenate([inverse, cubes], axis=0))
    for head in range(heads):
        gq_ref[head] = (
            turned[:, 0:1] * (gain_ref[head : head + 1] * dq_ref[head])
            - raw_ref[head].astype(F32) * turned[:, 2:3]
        ).astype(BF16)
        gk_ref[head] = (
            turned[:, 1:2] * (gain_ref[heads + head : heads + head + 1] * dk_ref[head])
            - raw_ref[heads + head].astype(F32) * turned[:, 3:4]
        ).astype(BF16)


SEQ, HEAD = ("x", "z"), ("y", "c")


def passed(value, steps):
    count = lax.axis_size("x") * lax.axis_size("z")
    pairs = [
        (2 * i + core, 2 * (i + way * steps) + core)
        for i in range(count)
        for core, way in enumerate((1, -1))
        if 0 <= i + way * steps < count
    ]
    return lax.ppermute(value, SEQ + ("c",), pairs)


def around(value, steps):
    count = lax.axis_size("x") * lax.axis_size("z")
    pairs = [
        (2 * i + core, 2 * ((i + way * steps) % count) + core)
        for i in range(count)
        for core, way in enumerate((1, -1))
    ]
    return lax.ppermute(value, SEQ + ("c",), pairs)


def relay(offset):
    return int(offset / 2) if abs(offset) > 2 else 0


def spread(value):
    got = {0: value}
    for offset in NEAR[1:]:
        got[offset] = passed(got[relay(offset)], relay(offset) - offset)
    return [got[offset] for offset in NEAR]


def collect(parts):
    near, line = len(NEAR), lax.axis_size("z")
    places = [near - 2, near - 1]
    carried = [parts[place] for place in places]
    stages = [
        lambda got: [
            passed(parts[1], NEAR[1]), passed(parts[2], NEAR[2]), around(parts[near + 2], -line)
        ],
        lambda got: [
            *got[:2],
            around((got[2].astype(F32) + parts[near]).astype(BF16), -line),
            passed(parts[near + 1], line),
        ],
    ]
    arrived = []
    while True:
        steps = [NEAR[place] - relay(NEAR[place]) for place in places]
        through = relay(NEAR[places[0]])
        carried = [passed(part, step) for part, step in zip(carried, steps)]
        if not through:
            break
        places = [place - 2 for place in places]
        carried = lax.optimization_barrier(carried)
        carried = [
            (part.astype(F32) + parts[place]).astype(BF16) for part, place in zip(carried, places)
        ]
        arrived = stages.pop(0)(arrived)
        carried, arrived = lax.optimization_barrier((carried, arrived))
    for stage in stages:
        arrived = stage(arrived)
    return arrived + carried


def per_device(total_heads, q_raw, k_raw, values, grad_out, q_gain, k_gain, key_tiles):
    line = lax.axis_size("z")
    groups = lax.axis_size("y") * lax.axis_size("c")
    near = len(NEAR)
    count = near + FAR
    heads = q_raw.shape[1]
    channels = float(total_heads * q_raw.shape[2])
    q_raw, k_raw, values, grad_out = [
        jnp.transpose(array, (1, 0, 2)) for array in (q_raw, k_raw, values, grad_out)
    ]
    gains = jnp.concatenate([q_gain, k_gain], axis=0)
    vmem = pl.BlockSpec(memory_space=pltpu.VMEM)
    params = pltpu.CompilerParams(vmem_limit_bytes=VMEM_LIMIT)
    whole, pair = (heads, TILE, TILE), (2 * heads, TILE, TILE)

    def call(kernel, name, out_shape, *operands):
        return pl.pallas_call(
            kernel,
            out_shape=[jax.ShapeDtypeStruct(shape, dtype) for shape, dtype in out_shape],
            in_specs=[vmem] * len(operands),
            out_specs=[vmem] * len(out_shape),
            compiler_params=params,
            name=name,
        )(*operands)

    rows = ((groups, 8, TILE), F32)
    raw = jnp.concatenate([q_raw, k_raw, values], axis=0)
    (squares,) = call(functools.partial(squares_kernel, heads), "squares", [rows], raw)
    sums = lax.all_to_all(squares, HEAD, 0, 0, tiled=True)
    q_norm, pairs, inverse = call(
        functools.partial(norm_kernel, heads, channels),
        "norm",
        [(whole, BF16), (pair, BF16), ((8, TILE), F32)],
        sums, gains, raw,
    )
    before = around(pairs, line)
    tiles = spread(pairs)
    tiles += [before, passed(pairs, -line), around(before, line)]
    late = [near - 2, near - 1]
    early = [t for t in range(count) if t not in late]
    early_tiles, late_tiles = [tiles[t] for t in early], [tiles[t] for t in late]
    square = ((TILE, TILE), F32)
    weights, early_out, early_rows = call(
        functools.partial(early_kernel, heads, early),
        "early",
        [((heads, len(early), TILE, TILE), F32), (whole, F32), square],
        q_norm, *early_tiles,
    )
    attended, late_dq, late_rows, *late_parts = call(
        functools.partial(late_kernel, heads, late),
        "late",
        [(whole, BF16), (whole, F32), square] + [(pair, BF16)] * len(late),
        q_norm, grad_out, early_out, early_rows, *late_tiles,
    )
    dq, *early_parts = call(
        functools.partial(rest_kernel, heads),
        "rest",
        [(whole, F32)] + [(pair, F32 if t == 0 or 2 < t <= near else BF16) for t in early],
        q_norm, grad_out, weights, late_dq, late_rows, *early_tiles,
    )
    parts = dict(zip(early + late, early_parts + late_parts))
    arrived = collect(parts)
    dk, grad_v, terms = call(
        functools.partial(terms_kernel, heads),
        "terms",
        [(whole, F32), (whole, BF16), rows],
        raw, dq, gains, parts[0], *arrived,
    )
    terms = lax.all_to_all(terms, HEAD, 0, 0, tiled=True)
    grad_q, grad_k = call(
        functools.partial(final_kernel, heads, channels),
        "final",
        [(whole, BF16)] * 2,
        inverse, terms, raw, dq, dk, gains,
    )
    return tuple(
        jnp.transpose(array, (1, 0, 2)) for array in (attended, grad_q, grad_k, grad_v)
    )


def solution(mesh):
    split = Mesh(mesh.devices.reshape(4, -1, mesh.shape["head"] // 2, 2), SEQ + HEAD)

    def whole(q_raw, k_raw, values, grad_out, q_gain, k_gain, key_tiles):
        tokens = P(SEQ, HEAD, None)
        return jax.shard_map(
            functools.partial(per_device, q_raw.shape[1]),
            mesh=split,
            in_specs=(tokens,) * 4 + (P(HEAD, None), P(HEAD, None), P()),
            out_specs=(tokens,) * 4,
            check_vma=False,
        )(q_raw, k_raw, values, grad_out, q_gain, k_gain, key_tiles)

    return whole
```

```python
import functools

import jax
import jax.numpy as jnp
from jax import lax
from jax.experimental import pallas as pl
from jax.experimental.pallas import tpu as pltpu
from jax.sharding import Mesh, PartitionSpec as P

TILE = 128
EPS = 1e-06
NEAR = (0, -1, 1, -2, 2, -4, 4, -8, 8)
FAR = 3
NT = (((1,), (1,)), ((), ()))
NN = (((1,), (0,)), ((), ()))
TN = (((0,), (0,)), ((), ()))
F32 = jnp.float32
BF16 = jnp.bfloat16
VMEM_LIMIT = 24 * 1024 * 1024


def dot(left, right, dims):
    return lax.dot_general(left, right, dims, preferred_element_type=F32)


def row_sums(square):
    ones = jnp.ones((8, TILE), BF16)
    high = square.astype(BF16)
    low = (square - high.astype(F32)).astype(BF16)
    return dot(ones, high, NT) + dot(ones, low, NT)


def columns(rows):
    fill = jnp.zeros((TILE - rows.shape[0], TILE), F32)
    return jnp.transpose(jnp.concatenate([rows, fill], axis=0))


def own_frame():
    return lax.axis_index("x") * lax.axis_size("z") + lax.axis_index("z")


def mirrored(value):
    return value * (1 - 2 * lax.axis_index("c"))


def inside(place):
    line, lines = lax.axis_size("z"), lax.axis_size("x")
    near = len(NEAR)
    if place == 0 or place == near + FAR - 1:
        return None
    offset = NEAR[place] if place < near else (-line, line)[place - near]
    at = own_frame() + mirrored(offset)
    return (at >= 0) & (at < line * lines)


def squares_kernel(heads, raw_ref, out_ref):
    out_ref[...] = jnp.zeros(out_ref.shape, F32)
    for row in range(2):
        total = jnp.zeros((TILE, TILE), F32)
        for head in range(heads):
            floats = raw_ref[row * heads + head].astype(F32)
            total = total + floats * floats
        total = row_sums(total)[0:1]
        for group in range(out_ref.shape[0]):
            out_ref[group, row : row + 1, :] = total


def group_sum(ref):
    total = ref[0]
    for group in range(1, ref.shape[0]):
        total = total + ref[group]
    return total


def norm_kernel(heads, channels, sums_ref, gain_ref, raw_ref, qn_ref, kv_ref, inverse_ref):
    inverse = lax.rsqrt(group_sum(sums_ref) / channels + EPS)
    inverse_ref[...] = inverse
    turned = columns(inverse)
    for head in range(heads):
        qn_ref[head] = (
            raw_ref[head].astype(F32) * turned[:, 0:1] * gain_ref[head : head + 1]
        ).astype(BF16)
        kv_ref[heads + head] = raw_ref[2 * heads + head]
        kv_ref[head] = (
            raw_ref[heads + head].astype(F32) * turned[:, 1:2] * gain_ref[heads + head : heads + head + 1]
        ).astype(BF16)


def early_kernel(heads, places, q_ref, *refs):
    tiles, (weight_ref, out_ref, rows_ref) = refs[: len(places)], refs[len(places) :]
    scale = TILE ** (-0.5)
    usable = [inside(place) for place in places]
    lane = lax.broadcasted_iota(jnp.int32, (TILE, TILE), 1)
    rows = jnp.zeros((TILE, TILE), F32)
    tops = []
    for head in range(heads):
        top = jnp.full((TILE, TILE), -1e30, F32)
        for t, tile in enumerate(tiles):
            score = dot(q_ref[head], tile[head], NT) * scale
            if usable[t] is not None:
                score = jnp.where(usable[t], score, -1e30)
            weight_ref[head, t] = score
            top = jnp.maximum(top, score)
        tops.append(jnp.max(top, axis=1, keepdims=True))
        rows = jnp.where(lane == head, tops[head], rows)
    for head in range(heads):
        total = jnp.zeros((TILE, TILE), F32)
        out = jnp.zeros((TILE, TILE), F32)
        for t, tile in enumerate(tiles):
            weight = jnp.exp(weight_ref[head, t] - tops[head])
            weight_ref[head, t] = weight
            total = total + weight
            out = out + dot(weight.astype(BF16), tile[heads + head], NN)
        out_ref[head] = out
        rows = jnp.where(lane == heads + head, jnp.sum(total, axis=1, keepdims=True), rows)
    rows_ref[...] = rows


def late_kernel(heads, places, q_ref, do_ref, early_ref, rows_ref, *refs):
    count = len(places)
    tiles = refs[:count]
    out_ref, dq_ref, late_rows_ref = refs[count : count + 3]
    part_refs = refs[count + 3 :]
    scale = TILE ** (-0.5)
    usable = [inside(place) for place in places]
    lane = lax.broadcasted_iota(jnp.int32, (TILE, TILE), 1)
    rows = jnp.zeros((TILE, TILE), F32)
    every = range(heads)
    scores = [
        [dot(q_ref[head], tile[head], NT) * scale for tile in tiles] for head in every
    ]
    scores = [
        [score if use is None else jnp.where(use, score, -1e30) for use, score in zip(usable, row)]
        for row in scores
    ]
    dprobs = [[dot(do_ref[head], tile[heads + head], NT) for tile in tiles] for head in every]
    weights, keeps, shares, outs, deltas = [], [], [], [], []
    for head in every:
        early_top = rows_ref[:, head : head + 1]
        top = scores[head][0]
        for score in scores[head][1:]:
            top = jnp.maximum(top, score)
        top = jnp.maximum(early_top, jnp.max(top, axis=1, keepdims=True))
        keeps.append(jnp.exp(early_top - top))
        weights.append([jnp.exp(score - top) for score in scores[head]])
        total = weights[head][0]
        for weight in weights[head][1:]:
            total = total + weight
        total = jnp.sum(total, axis=1, keepdims=True)
        total = total + rows_ref[:, heads + head : heads + head + 1] * keeps[head]
        shares.append(1.0 / total)
    for head in every:
        out = early_ref[head] * keeps[head]
        for weight, tile in zip(weights[head], tiles):
            out = out + dot(weight.astype(BF16), tile[heads + head], NN)
        outs.append((out * shares[head]).astype(BF16))
        deltas.append(
            jnp.sum(do_ref[head].astype(F32) * outs[head].astype(F32), axis=1, keepdims=True)
        )
    probs = [[weight * shares[head] for weight in weights[head]] for head in every]
    dscores = [
        [(prob * (dprob - deltas[head])).astype(BF16) for prob, dprob in zip(probs[head], dprobs[head])]
        for head in every
    ]
    value_parts = [[dot(prob.astype(BF16), do_ref[head], TN) for prob in probs[head]] for head in every]
    key_parts = [[dot(dscore, q_ref[head], TN) * scale for dscore in dscores[head]] for head in every]
    for head in every:
        query_grad = jnp.zeros((TILE, TILE), F32)
        for dscore, tile in zip(dscores[head], tiles):
            query_grad = query_grad + dot(dscore, tile[head], NN)
        rows = jnp.where(lane == head, keeps[head] * shares[head], rows)
        rows = jnp.where(lane == heads + head, deltas[head], rows)
        for t, part in enumerate(part_refs):
            part[head] = key_parts[head][t].astype(part.dtype)
            part[heads + head] = value_parts[head][t].astype(part.dtype)
        out_ref[head] = outs[head]
        dq_ref[head] = query_grad
    late_rows_ref[...] = rows


def rest_kernel(heads, q_ref, do_ref, weight_ref, late_dq_ref, rows_ref, *refs):
    count = (len(refs) - 1) // 2
    tiles, dq_ref, part_refs = refs[:count], refs[count], refs[count + 1 :]
    scale = TILE ** (-0.5)
    for head in range(heads):
        query, upstream = q_ref[head], do_ref[head]
        share = rows_ref[:, head : head + 1]
        delta = rows_ref[:, heads + head : heads + head + 1]
        dprobs = [dot(upstream, tile[heads + head], NT) for tile in tiles]
        probs = [weight_ref[head, t] * share for t in range(count)]
        dscores = [(prob * (dprob - delta)).astype(BF16) for prob, dprob in zip(probs, dprobs)]
        query_grad = late_dq_ref[head]
        for dscore, tile in zip(dscores, tiles):
            query_grad = query_grad + dot(dscore, tile[head], NN)
        value_parts = [dot(prob.astype(BF16), upstream, TN) for prob in probs]
        key_parts = [dot(dscore, query, TN) * scale for dscore in dscores]
        for part, key_part, value_part in zip(part_refs, key_parts, value_parts):
            part[head] = key_part.astype(part.dtype)
            part[heads + head] = value_part.astype(part.dtype)
        dq_ref[head] = query_grad * scale


def terms_kernel(heads, raw_ref, dq_ref, gain_ref, *refs):
    parts, (dk_ref, dv_ref, terms_ref) = refs[:-3], refs[-3:]
    query_total = jnp.zeros((TILE, TILE), F32)
    key_total = jnp.zeros((TILE, TILE), F32)
    for head in range(heads):
        key_grad, value_grad = parts[0][head], parts[0][heads + head]
        for part in parts[1:]:
            key_grad = key_grad + part[head].astype(F32)
            value_grad = value_grad + part[heads + head].astype(F32)
        dk_ref[head] = key_grad
        dv_ref[head] = value_grad.astype(BF16)
        query_total = query_total + raw_ref[head].astype(F32) * (
            dq_ref[head] * gain_ref[head : head + 1]
        )
        key_total = key_total + raw_ref[heads + head].astype(F32) * (
            key_grad * gain_ref[heads + head : heads + head + 1]
        )
    terms_ref[...] = jnp.zeros(terms_ref.shape, F32)
    for row, total in enumerate((query_total, key_total)):
        total = row_sums(total)[0:1]
        for group in range(terms_ref.shape[0]):
            terms_ref[group, row : row + 1, :] = total


def final_kernel(
    heads, channels, inverse_ref, terms_ref, raw_ref, dq_ref, dk_ref, gain_ref, gq_ref, gk_ref
):
    inverse = inverse_ref[0:2]
    cubes = inverse * inverse * inverse * group_sum(terms_ref)[0:2] / channels
    turned = columns(jnp.concatenate([inverse, cubes], axis=0))
    for head in range(heads):
        gq_ref[head] = (
            turned[:, 0:1] * (gain_ref[head : head + 1] * dq_ref[head])
            - raw_ref[head].astype(F32) * turned[:, 2:3]
        ).astype(BF16)
        gk_ref[head] = (
            turned[:, 1:2] * (gain_ref[heads + head : heads + head + 1] * dk_ref[head])
            - raw_ref[heads + head].astype(F32) * turned[:, 3:4]
        ).astype(BF16)


SEQ, HEAD = ("x", "z"), ("y", "c")


def passed(value, steps):
    count = lax.axis_size("x") * lax.axis_size("z")
    pairs = [
        (2 * i + core, 2 * (i + way * steps) + core)
        for i in range(count)
        for core, way in enumerate((1, -1))
        if 0 <= i + way * steps < count
    ]
    return lax.ppermute(value, SEQ + ("c",), pairs)


def around(value, steps):
    count = lax.axis_size("x") * lax.axis_size("z")
    pairs = [
        (2 * i + core, 2 * ((i + way * steps) % count) + core)
        for i in range(count)
        for core, way in enumerate((1, -1))
    ]
    return lax.ppermute(value, SEQ + ("c",), pairs)


def relay(offset):
    return int(offset / 2) if abs(offset) > 2 else 0


def spread(value):
    got = {0: value}
    for offset in NEAR[1:]:
        got[offset] = passed(got[relay(offset)], relay(offset) - offset)
    return [got[offset] for offset in NEAR]


def collect(parts):
    near, line = len(NEAR), lax.axis_size("z")
    places = [near - 2, near - 1]
    carried = [parts[place] for place in places]
    stages = [
        lambda got: [
            passed(parts[1], NEAR[1]), passed(parts[2], NEAR[2]), around(parts[near + 2], -line)
        ],
        lambda got: [
            *got[:2],
            around((got[2].astype(F32) + parts[near]).astype(BF16), -line),
            passed(parts[near + 1], line),
        ],
    ]
    arrived = []
    while True:
        steps = [NEAR[place] - relay(NEAR[place]) for place in places]
        through = relay(NEAR[places[0]])
        carried = [passed(part, step) for part, step in zip(carried, steps)]
        if not through:
            break
        places = [place - 2 for place in places]
        carried = lax.optimization_barrier(carried)
        carried = [
            (part.astype(F32) + parts[place]).astype(BF16) for part, place in zip(carried, places)
        ]
        arrived = stages.pop(0)(arrived)
        carried, arrived = lax.optimization_barrier((carried, arrived))
    for stage in stages:
        arrived = stage(arrived)
    return arrived + carried


def per_device(total_heads, q_raw, k_raw, values, grad_out, q_gain, k_gain, key_tiles):
    line = lax.axis_size("z")
    groups = lax.axis_size("y") * lax.axis_size("c")
    near = len(NEAR)
    count = near + FAR
    heads = q_raw.shape[1]
    channels = float(total_heads * q_raw.shape[2])
    q_raw, k_raw, values, grad_out = [
        jnp.transpose(array, (1, 0, 2)) for array in (q_raw, k_raw, values, grad_out)
    ]
    gains = jnp.concatenate([q_gain, k_gain], axis=0)
    vmem = pl.BlockSpec(memory_space=pltpu.VMEM)
    params = pltpu.CompilerParams(vmem_limit_bytes=VMEM_LIMIT)
    whole, pair = (heads, TILE, TILE), (2 * heads, TILE, TILE)

    def call(kernel, name, out_shape, *operands):
        return pl.pallas_call(
            kernel,
            out_shape=[jax.ShapeDtypeStruct(shape, dtype) for shape, dtype in out_shape],
            in_specs=[vmem] * len(operands),
            out_specs=[vmem] * len(out_shape),
            compiler_params=params,
            name=name,
        )(*operands)

    rows = ((groups, 8, TILE), F32)
    raw = jnp.concatenate([q_raw, k_raw, values], axis=0)
    (squares,) = call(functools.partial(squares_kernel, heads), "squares", [rows], raw)
    sums = lax.all_to_all(squares, HEAD, 0, 0, tiled=True)
    q_norm, pairs, inverse = call(
        functools.partial(norm_kernel, heads, channels),
        "norm",
        [(whole, BF16), (pair, BF16), ((8, TILE), F32)],
        sums, gains, raw,
    )
    before = around(pairs, line)
    tiles = spread(pairs)
    tiles += [before, passed(pairs, -line), None]
    late = [near - 2, near - 1, near + 2]
    early = [t for t in range(count) if t not in late]
    early_tiles = [tiles[t] for t in early]
    square = ((TILE, TILE), F32)
    weights, early_out, early_rows = call(
        functools.partial(early_kernel, heads, early),
        "early",
        [((heads, len(early), TILE, TILE), F32), (whole, F32), square],
        q_norm, *early_tiles,
    )
    before, early_rows = lax.optimization_barrier((before, early_rows))
    tiles[near + 2] = around(before, line)
    late_tiles = [tiles[t] for t in late]
    attended, late_dq, late_rows, *late_parts = call(
        functools.partial(late_kernel, heads, late),
        "late",
        [(whole, BF16), (whole, F32), square] + [(pair, BF16)] * len(late),
        q_norm, grad_out, early_out, early_rows, *late_tiles,
    )
    dq, *early_parts = call(
        functools.partial(rest_kernel, heads),
        "rest",
        [(whole, F32)] + [(pair, F32 if t == 0 or 2 < t <= near else BF16) for t in early],
        q_norm, grad_out, weights, late_dq, late_rows, *early_tiles,
    )
    parts = dict(zip(early + late, early_parts + late_parts))
    arrived = collect(parts)
    dk, grad_v, terms = call(
        functools.partial(terms_kernel, heads),
        "terms",
        [(whole, F32), (whole, BF16), rows],
        raw, dq, gains, parts[0], *arrived,
    )
    terms = lax.all_to_all(terms, HEAD, 0, 0, tiled=True)
    grad_q, grad_k = call(
        functools.partial(final_kernel, heads, channels),
        "final",
        [(whole, BF16)] * 2,
        inverse, terms, raw, dq, dk, gains,
    )
    return tuple(
        jnp.transpose(array, (1, 0, 2)) for array in (attended, grad_q, grad_k, grad_v)
    )


def solution(mesh):
    split = Mesh(mesh.devices.reshape(4, -1, mesh.shape["head"] // 2, 2), SEQ + HEAD)

    def whole(q_raw, k_raw, values, grad_out, q_gain, k_gain, key_tiles):
        tokens = P(SEQ, HEAD, None)
        return jax.shard_map(
            functools.partial(per_device, q_raw.shape[1]),
            mesh=split,
            in_specs=(tokens,) * 4 + (P(HEAD, None), P(HEAD, None), P()),
            out_specs=(tokens,) * 4,
            check_vma=False,
        )(q_raw, k_raw, values, grad_out, q_gain, k_gain, key_tiles)

    return whole
```

```python
import functools

import jax
import jax.numpy as jnp
from jax import lax
from jax.experimental import pallas as pl
from jax.experimental.pallas import tpu as pltpu
from jax.sharding import Mesh, PartitionSpec as P

TILE = 128
EPS = 1e-06
NEAR = (0, -1, 1, -2, 2, -4, 4, -8, 8)
FAR = 3
NT = (((1,), (1,)), ((), ()))
NN = (((1,), (0,)), ((), ()))
TN = (((0,), (0,)), ((), ()))
F32 = jnp.float32
BF16 = jnp.bfloat16
VMEM_LIMIT = 24 * 1024 * 1024


def dot(left, right, dims):
    return lax.dot_general(left, right, dims, preferred_element_type=F32)


def row_sums(square):
    ones = jnp.ones((8, TILE), BF16)
    high = square.astype(BF16)
    low = (square - high.astype(F32)).astype(BF16)
    return dot(ones, high, NT) + dot(ones, low, NT)


def columns(rows):
    fill = jnp.zeros((TILE - rows.shape[0], TILE), F32)
    return jnp.transpose(jnp.concatenate([rows, fill], axis=0))


def own_frame():
    return lax.axis_index("x") * lax.axis_size("z") + lax.axis_index("z")


def mirrored(value):
    return value * (1 - 2 * lax.axis_index("c"))


def inside(place):
    line, lines = lax.axis_size("z"), lax.axis_size("x")
    near = len(NEAR)
    if place == 0 or place == near + FAR - 1:
        return None
    offset = NEAR[place] if place < near else (-line, line)[place - near]
    at = own_frame() + mirrored(offset)
    return (at >= 0) & (at < line * lines)


def squares_kernel(heads, raw_ref, out_ref):
    out_ref[...] = jnp.zeros(out_ref.shape, F32)
    for row in range(2):
        total = jnp.zeros((TILE, TILE), F32)
        for head in range(heads):
            floats = raw_ref[row * heads + head].astype(F32)
            total = total + floats * floats
        total = row_sums(total)[0:1]
        for group in range(out_ref.shape[0]):
            out_ref[group, row : row + 1, :] = total


def group_sum(ref):
    total = ref[0]
    for group in range(1, ref.shape[0]):
        total = total + ref[group]
    return total


def norm_kernel(heads, channels, sums_ref, gain_ref, raw_ref, qn_ref, kv_ref, inverse_ref):
    inverse = lax.rsqrt(group_sum(sums_ref) / channels + EPS)
    inverse_ref[...] = inverse
    turned = columns(inverse)
    for head in range(heads):
        qn_ref[head] = (
            raw_ref[head].astype(F32) * turned[:, 0:1] * gain_ref[head : head + 1]
        ).astype(BF16)
        kv_ref[heads + head] = raw_ref[2 * heads + head]
        kv_ref[head] = (
            raw_ref[heads + head].astype(F32) * turned[:, 1:2] * gain_ref[heads + head : heads + head + 1]
        ).astype(BF16)


def early_kernel(heads, places, q_ref, *refs):
    tiles, (weight_ref, out_ref, rows_ref) = refs[: len(places)], refs[len(places) :]
    scale = TILE ** (-0.5)
    usable = [inside(place) for place in places]
    lane = lax.broadcasted_iota(jnp.int32, (TILE, TILE), 1)
    rows = jnp.zeros((TILE, TILE), F32)
    tops = []
    for head in range(heads):
        top = jnp.full((TILE, TILE), -1e30, F32)
        for t, tile in enumerate(tiles):
            score = dot(q_ref[head], tile[head], NT) * scale
            if usable[t] is not None:
                score = jnp.where(usable[t], score, -1e30)
            weight_ref[head, t] = score
            top = jnp.maximum(top, score)
        tops.append(jnp.max(top, axis=1, keepdims=True))
        rows = jnp.where(lane == head, tops[head], rows)
    for head in range(heads):
        total = jnp.zeros((TILE, TILE), F32)
        out = jnp.zeros((TILE, TILE), F32)
        for t, tile in enumerate(tiles):
            weight = jnp.exp(weight_ref[head, t] - tops[head])
            weight_ref[head, t] = weight
            total = total + weight
            out = out + dot(weight.astype(BF16), tile[heads + head], NN)
        out_ref[head] = out
        rows = jnp.where(lane == heads + head, jnp.sum(total, axis=1, keepdims=True), rows)
    rows_ref[...] = rows


def late_kernel(heads, places, q_ref, do_ref, early_ref, rows_ref, *refs):
    count = len(places)
    tiles = refs[:count]
    out_ref, dq_ref, late_rows_ref = refs[count : count + 3]
    part_refs = refs[count + 3 :]
    scale = TILE ** (-0.5)
    usable = [inside(place) for place in places]
    lane = lax.broadcasted_iota(jnp.int32, (TILE, TILE), 1)
    rows = jnp.zeros((TILE, TILE), F32)
    every = range(heads)
    scores = [
        [dot(q_ref[head], tile[head], NT) * scale for tile in tiles] for head in every
    ]
    scores = [
        [score if use is None else jnp.where(use, score, -1e30) for use, score in zip(usable, row)]
        for row in scores
    ]
    dprobs = [[dot(do_ref[head], tile[heads + head], NT) for tile in tiles] for head in every]
    weights, keeps, shares, outs, deltas = [], [], [], [], []
    for head in every:
        early_top = rows_ref[:, head : head + 1]
        top = scores[head][0]
        for score in scores[head][1:]:
            top = jnp.maximum(top, score)
        top = jnp.maximum(early_top, jnp.max(top, axis=1, keepdims=True))
        keeps.append(jnp.exp(early_top - top))
        weights.append([jnp.exp(score - top) for score in scores[head]])
        total = weights[head][0]
        for weight in weights[head][1:]:
            total = total + weight
        total = jnp.sum(total, axis=1, keepdims=True)
        total = total + rows_ref[:, heads + head : heads + head + 1] * keeps[head]
        shares.append(1.0 / total)
    for head in every:
        out = early_ref[head] * keeps[head]
        for weight, tile in zip(weights[head], tiles):
            out = out + dot(weight.astype(BF16), tile[heads + head], NN)
        outs.append((out * shares[head]).astype(BF16))
        deltas.append(
            jnp.sum(do_ref[head].astype(F32) * outs[head].astype(F32), axis=1, keepdims=True)
        )
    probs = [[weight * shares[head] for weight in weights[head]] for head in every]
    dscores = [
        [(prob * (dprob - deltas[head])).astype(BF16) for prob, dprob in zip(probs[head], dprobs[head])]
        for head in every
    ]
    value_parts = [[dot(prob.astype(BF16), do_ref[head], TN) for prob in probs[head]] for head in every]
    key_parts = [[dot(dscore, q_ref[head], TN) * scale for dscore in dscores[head]] for head in every]
    for head in every:
        query_grad = jnp.zeros((TILE, TILE), F32)
        for dscore, tile in zip(dscores[head], tiles):
            query_grad = query_grad + dot(dscore, tile[head], NN)
        rows = jnp.where(lane == head, keeps[head] * shares[head], rows)
        rows = jnp.where(lane == heads + head, deltas[head], rows)
        for t, part in enumerate(part_refs):
            part[head] = key_parts[head][t].astype(part.dtype)
            part[heads + head] = value_parts[head][t].astype(part.dtype)
        out_ref[head] = outs[head]
        dq_ref[head] = query_grad
    late_rows_ref[...] = rows


def rest_kernel(heads, q_ref, do_ref, weight_ref, late_dq_ref, rows_ref, *refs):
    count = (len(refs) - 1) // 2
    tiles, dq_ref, part_refs = refs[:count], refs[count], refs[count + 1 :]
    scale = TILE ** (-0.5)
    for head in range(heads):
        query, upstream = q_ref[head], do_ref[head]
        share = rows_ref[:, head : head + 1]
        delta = rows_ref[:, heads + head : heads + head + 1]
        dprobs = [dot(upstream, tile[heads + head], NT) for tile in tiles]
        probs = [weight_ref[head, t] * share for t in range(count)]
        dscores = [(prob * (dprob - delta)).astype(BF16) for prob, dprob in zip(probs, dprobs)]
        query_grad = late_dq_ref[head]
        for dscore, tile in zip(dscores, tiles):
            query_grad = query_grad + dot(dscore, tile[head], NN)
        value_parts = [dot(prob.astype(BF16), upstream, TN) for prob in probs]
        key_parts = [dot(dscore, query, TN) * scale for dscore in dscores]
        for part, key_part, value_part in zip(part_refs, key_parts, value_parts):
            part[head] = key_part.astype(part.dtype)
            part[heads + head] = value_part.astype(part.dtype)
        dq_ref[head] = query_grad * scale


def terms_kernel(heads, raw_ref, dq_ref, gain_ref, *refs):
    parts, (dk_ref, dv_ref, terms_ref) = refs[:-3], refs[-3:]
    query_total = jnp.zeros((TILE, TILE), F32)
    key_total = jnp.zeros((TILE, TILE), F32)
    for head in range(heads):
        key_grad, value_grad = parts[0][head], parts[0][heads + head]
        for part in parts[1:]:
            key_grad = key_grad + part[head].astype(F32)
            value_grad = value_grad + part[heads + head].astype(F32)
        dk_ref[head] = key_grad
        dv_ref[head] = value_grad.astype(BF16)
        query_total = query_total + raw_ref[head].astype(F32) * (
            dq_ref[head] * gain_ref[head : head + 1]
        )
        key_total = key_total + raw_ref[heads + head].astype(F32) * (
            key_grad * gain_ref[heads + head : heads + head + 1]
        )
    terms_ref[...] = jnp.zeros(terms_ref.shape, F32)
    for row, total in enumerate((query_total, key_total)):
        total = row_sums(total)[0:1]
        for group in range(terms_ref.shape[0]):
            terms_ref[group, row : row + 1, :] = total


def final_kernel(
    heads, channels, inverse_ref, terms_ref, raw_ref, dq_ref, dk_ref, gain_ref, gq_ref, gk_ref
):
    inverse = inverse_ref[0:2]
    cubes = inverse * inverse * inverse * group_sum(terms_ref)[0:2] / channels
    turned = columns(jnp.concatenate([inverse, cubes], axis=0))
    for head in range(heads):
        gq_ref[head] = (
            turned[:, 0:1] * (gain_ref[head : head + 1] * dq_ref[head])
            - raw_ref[head].astype(F32) * turned[:, 2:3]
        ).astype(BF16)
        gk_ref[head] = (
            turned[:, 1:2] * (gain_ref[heads + head : heads + head + 1] * dk_ref[head])
            - raw_ref[heads + head].astype(F32) * turned[:, 3:4]
        ).astype(BF16)


SEQ, HEAD = ("x", "z"), ("y", "c")


def passed(value, steps):
    count = lax.axis_size("x") * lax.axis_size("z")
    pairs = [
        (2 * i + core, 2 * (i + way * steps) + core)
        for i in range(count)
        for core, way in enumerate((1, -1))
        if 0 <= i + way * steps < count
    ]
    return lax.ppermute(value, SEQ + ("c",), pairs)


def around(value, steps):
    count = lax.axis_size("x") * lax.axis_size("z")
    pairs = [
        (2 * i + core, 2 * ((i + way * steps) % count) + core)
        for i in range(count)
        for core, way in enumerate((1, -1))
    ]
    return lax.ppermute(value, SEQ + ("c",), pairs)


def relay(offset):
    return int(offset / 2) if abs(offset) > 2 else 0


def spread(value):
    got = {0: value}
    for offset in NEAR[1:]:
        got[offset] = passed(got[relay(offset)], relay(offset) - offset)
    return [got[offset] for offset in NEAR]


def collect(parts):
    near, line = len(NEAR), lax.axis_size("z")
    places = [near - 2, near - 1]
    carried = [parts[place] for place in places]
    stages = [
        lambda got: [
            passed(parts[1], NEAR[1]), passed(parts[2], NEAR[2]), around(parts[near + 2], -line)
        ],
        lambda got: [
            *got[:2],
            around((got[2].astype(F32) + parts[near]).astype(BF16), -line),
            passed(parts[near + 1], line),
        ],
    ]
    arrived = []
    while True:
        steps = [NEAR[place] - relay(NEAR[place]) for place in places]
        through = relay(NEAR[places[0]])
        carried = [passed(part, step) for part, step in zip(carried, steps)]
        if not through:
            break
        places = [place - 2 for place in places]
        carried = lax.optimization_barrier(carried)
        carried = [
            (part.astype(F32) + parts[place]).astype(BF16) for part, place in zip(carried, places)
        ]
        arrived = stages.pop(0)(arrived)
        carried, arrived = lax.optimization_barrier((carried, arrived))
    for stage in stages:
        arrived = stage(arrived)
    return arrived + carried


def per_device(total_heads, q_raw, k_raw, values, grad_out, q_gain, k_gain, key_tiles):
    line = lax.axis_size("z")
    groups = lax.axis_size("y") * lax.axis_size("c")
    near = len(NEAR)
    count = near + FAR
    heads = q_raw.shape[1]
    channels = float(total_heads * q_raw.shape[2])
    q_raw, k_raw, values, grad_out = [
        jnp.transpose(array, (1, 0, 2)) for array in (q_raw, k_raw, values, grad_out)
    ]
    gains = jnp.concatenate([q_gain, k_gain], axis=0)
    vmem = pl.BlockSpec(memory_space=pltpu.VMEM)
    params = pltpu.CompilerParams(vmem_limit_bytes=VMEM_LIMIT)
    whole, pair = (heads, TILE, TILE), (2 * heads, TILE, TILE)

    def call(kernel, name, out_shape, *operands):
        return pl.pallas_call(
            kernel,
            out_shape=[jax.ShapeDtypeStruct(shape, dtype) for shape, dtype in out_shape],
            in_specs=[vmem] * len(operands),
            out_specs=[vmem] * len(out_shape),
            compiler_params=params,
            name=name,
        )(*operands)

    rows = ((groups, 8, TILE), F32)
    raw = jnp.concatenate([q_raw, k_raw, values], axis=0)
    (squares,) = call(functools.partial(squares_kernel, heads), "squares", [rows], raw)
    sums = lax.all_to_all(squares, HEAD, 0, 0, tiled=True)
    q_norm, pairs, inverse = call(
        functools.partial(norm_kernel, heads, channels),
        "norm",
        [(whole, BF16), (pair, BF16), ((8, TILE), F32)],
        sums, gains, raw,
    )
    before = around(pairs, line)
    tiles = spread(pairs)
    tiles += [before, passed(pairs, -line), around(before, line)]
    late = [near - 2, near - 1]
    early = [0, near, near + 1, *range(3, near - 2), 1, 2, near + 2]
    early_tiles, late_tiles = [tiles[t] for t in early], [tiles[t] for t in late]
    square = ((TILE, TILE), F32)
    weights, early_out, early_rows = call(
        functools.partial(early_kernel, heads, early),
        "early",
        [((heads, len(early), TILE, TILE), F32), (whole, F32), square],
        q_norm, *early_tiles,
    )
    attended, late_dq, late_rows, *late_parts = call(
        functools.partial(late_kernel, heads, late),
        "late",
        [(whole, BF16), (whole, F32), square] + [(pair, BF16)] * len(late),
        q_norm, grad_out, early_out, early_rows, *late_tiles,
    )
    dq, *early_parts = call(
        functools.partial(rest_kernel, heads),
        "rest",
        [(whole, F32)] + [(pair, F32 if t == 0 or 2 < t <= near else BF16) for t in early],
        q_norm, grad_out, weights, late_dq, late_rows, *early_tiles,
    )
    parts = dict(zip(early + late, early_parts + late_parts))
    arrived = collect(parts)
    dk, grad_v, terms = call(
        functools.partial(terms_kernel, heads),
        "terms",
        [(whole, F32), (whole, BF16), rows],
        raw, dq, gains, parts[0], *arrived,
    )
    terms = lax.all_to_all(terms, HEAD, 0, 0, tiled=True)
    grad_q, grad_k = call(
        functools.partial(final_kernel, heads, channels),
        "final",
        [(whole, BF16)] * 2,
        inverse, terms, raw, dq, dk, gains,
    )
    return tuple(
        jnp.transpose(array, (1, 0, 2)) for array in (attended, grad_q, grad_k, grad_v)
    )


def solution(mesh):
    split = Mesh(mesh.devices.reshape(4, -1, mesh.shape["head"] // 2, 2), SEQ + HEAD)

    def whole(q_raw, k_raw, values, grad_out, q_gain, k_gain, key_tiles):
        tokens = P(SEQ, HEAD, None)
        return jax.shard_map(
            functools.partial(per_device, q_raw.shape[1]),
            mesh=split,
            in_specs=(tokens,) * 4 + (P(HEAD, None), P(HEAD, None), P()),
            out_specs=(tokens,) * 4,
            check_vma=False,
        )(q_raw, k_raw, values, grad_out, q_gain, k_gain, key_tiles)

    return whole
```
